256 devices in a mesh: row: 8 (over y, z_lo), col: 16 (over z_hi, x), seq: 2 (over core).
Axes of the slice: x: 4, y: 4, z: 8 (z_hi: 4, z_lo: 2; z = z_hi * 2 + z_lo), core: 2. Of those that a mesh axis runs over, the one named last changes fastest.
Arguments:
- pair: float32 [256, 256, 128], P('row', ('col', 'seq')), may hold values from -6 to 6
- alignment_left: float32 [128, 256, 32], P('seq', 'row', 'col'), may hold values from -6 to 6
- alignment_right: float32 [128, 256, 32], P('seq', 'col', 'row'), may hold values from -6 to 6
- outer_mean_weight: float32 [1024, 128], replicated, may hold values from -4 to 4
- outer_mean_bias: float32 [128], replicated, may hold values from -192 to 192
- input_norm_gain: float32 [128], replicated, may hold values from 0.1 to 1.9
- input_norm_bias: float32 [128], replicated, may hold values from -4 to 4
- input_weight_matrix: float32 [128, 640], replicated, may hold values from -0.5 to 0.5
- input_bias_vector: float32 [640], replicated, may hold values from -4 to 4
- output_norm_gain: float32 [128], replicated, may hold values from 0.1 to 1.9
- output_norm_bias: float32 [128], replicated, may hold values from -4 to 4
- output_weight_matrix: float32 [128, 128], replicated, may hold values from -0.5 to 0.5
- output_bias_vector: float32 [128], replicated, may hold values from -4 to 4
Outputs:
- pair_out: float32 [256, 256, 128], P('row', ('col', 'seq'))
The draws below stay inside these ranges and needn't reach their ends.
All inputs are finite; a program needn't handle non-finite values.
Results may differ from the reference program's by a relative error of at most 0.000064.
Values sent between devices are 32-bit elements; how exact they have to be, the bound alone decides.
No kernel may reach another device: no remote copies, remote signals or barrier semaphores. Data moves between devices by JAX's collectives and lax.ppermute only.
A program may use at most 64 MiB of HBM per device.

```python
import jax
import jax.numpy as jnp
from jax import lax

C = 128
PROJECTED_DIM = 32
SEQUENCE_COUNT = 128
RESIDUE_COUNT = 256


def steps_of(stream_key, extent, cuts, least, largest):
    level = 1.0
    for axis_at, blocks in cuts:
        heights = jax.random.uniform(jax.random.fold_in(jax.random.fold_in(stream_key, 6), axis_at), (blocks,), jnp.float32, least / len(cuts), largest / len(cuts))
        level = level * jnp.repeat(jnp.exp(heights), extent[axis_at] // blocks).reshape((-1,) + (1,) * (len(extent) - 1 - axis_at))
    return level


def normal_values(rng, dims, width, bound, split=(), kind=jnp.bfloat16):
    level = steps_of(rng, dims, split, -0.22, 0.18) if split else 1.0
    values = jax.random.normal(rng, dims, jnp.float32) * width * level
    return jnp.minimum(jnp.maximum(values, -bound), bound).astype(kind)


def setup_inputs(seed: int = 0) -> dict:
    key_of = jax.random.split(jax.random.key(seed), 14)
    pair = normal_values(key_of[0], (RESIDUE_COUNT, RESIDUE_COUNT, C), 1.0, 6.0, ((0, 8), (1, 32)), jnp.float32)
    alignment_left = normal_values(key_of[1], (SEQUENCE_COUNT, RESIDUE_COUNT, PROJECTED_DIM), 1.0, 6.0, ((0, 2), (1, 8), (2, 16)), jnp.float32)
    alignment_right = normal_values(key_of[2], (SEQUENCE_COUNT, RESIDUE_COUNT, PROJECTED_DIM), 1.0, 6.0, ((0, 2), (1, 16), (2, 8)), jnp.float32)
    outer_mean_weight = normal_values(key_of[3], (PROJECTED_DIM * PROJECTED_DIM, C), 0.3, 4.0, (), jnp.float32)
    outer_mean_bias = normal_values(key_of[4], (C,), (0.25 * SEQUENCE_COUNT), 192.0, (), jnp.float32)
    input_norm_gain = jnp.clip(1.0 + 0.18 * jax.random.normal(key_of[5], (C,), jnp.float32), 0.1, 1.9)
    input_norm_bias = normal_values(key_of[6], (C,), 0.3, 4.0, (), jnp.float32)
    input_weight_matrix = normal_values(key_of[7], (C, 5 * C), C ** -0.5, 0.5, (), jnp.float32)
    input_bias_vector = normal_values(key_of[8], (5 * C,), 0.5, 4.0, (), jnp.float32)
    output_norm_gain = jnp.clip(1.0 + 0.18 * jax.random.normal(key_of[9], (C,), jnp.float32), 0.1, 1.9)
    output_norm_bias = normal_values(key_of[10], (C,), 0.3, 4.0, (), jnp.float32)
    output_weight_matrix = normal_values(key_of[11], (C, C), C ** -0.5, 0.5, (), jnp.float32)
    output_bias_vector = normal_values(key_of[12], (C,), 0.5, 4.0, (), jnp.float32)
    return dict(pair=pair, alignment_left=alignment_left, alignment_right=alignment_right, outer_mean_weight=outer_mean_weight, outer_mean_bias=outer_mean_bias, input_norm_gain=input_norm_gain, input_norm_bias=input_norm_bias, input_weight_matrix=input_weight_matrix, input_bias_vector=input_bias_vector, output_norm_gain=output_norm_gain, output_norm_bias=output_norm_bias, output_weight_matrix=output_weight_matrix, output_bias_vector=output_bias_vector)


def layer_norm(values, gain, shift):
    center = values - lax.optimization_barrier(jnp.mean(values, axis=-1, keepdims=True))
    spread = lax.optimization_barrier(jnp.mean(center * center, axis=-1, keepdims=True))
    return center * lax.rsqrt(spread + 1e-05) * gain + shift

def reference(pair, alignment_left, alignment_right, outer_mean_weight, outer_mean_bias, input_norm_gain, input_norm_bias, input_weight_matrix, input_bias_vector, output_norm_gain, output_norm_bias, output_weight_matrix, output_bias_vector):
    highest = lax.Precision.HIGHEST
    stride_amount = 32
    block_list = alignment_left.reshape(SEQUENCE_COUNT, RESIDUE_COUNT // stride_amount, stride_amount, PROJECTED_DIM).transpose(1, 0, 2, 3)
    right_flattened = alignment_right.reshape(SEQUENCE_COUNT, RESIDUE_COUNT * PROJECTED_DIM)

    def one_block(left_block):
        outer = jnp.dot(left_block.reshape(SEQUENCE_COUNT, stride_amount * PROJECTED_DIM).T, right_flattened, precision=highest)
        outer = outer.reshape(stride_amount, PROJECTED_DIM, RESIDUE_COUNT, PROJECTED_DIM).transpose(0, 2, 1, 3).reshape(stride_amount * RESIDUE_COUNT, PROJECTED_DIM * PROJECTED_DIM)
        return jnp.dot(outer, outer_mean_weight, precision=highest).reshape(stride_amount, RESIDUE_COUNT, C)
    summed = lax.map(one_block, block_list).reshape(RESIDUE_COUNT, RESIDUE_COUNT, C)
    updated = pair + (summed + outer_mean_bias) / SEQUENCE_COUNT
    normed = layer_norm(updated, input_norm_gain, input_norm_bias)
    proj = jnp.dot(normed.reshape(RESIDUE_COUNT * RESIDUE_COUNT, C), input_weight_matrix, precision=highest) + input_bias_vector
    left_act = (jax.nn.sigmoid(proj[:, C:2 * C]) * proj[:, :C]).reshape(RESIDUE_COUNT, RESIDUE_COUNT, C)
    right_act = (jax.nn.sigmoid(proj[:, 3 * C:4 * C]) * proj[:, 2 * C:3 * C]).reshape(RESIDUE_COUNT, RESIDUE_COUNT, C)
    gate = jax.nn.sigmoid(proj[:, 4 * C:]).reshape(RESIDUE_COUNT, RESIDUE_COUNT, C)
    mixed = jnp.einsum('kic,kjc->ijc', left_act, right_act, precision=highest)
    normed_out = layer_norm(mixed, output_norm_gain, output_norm_bias)
    result = jnp.dot(normed_out.reshape(RESIDUE_COUNT * RESIDUE_COUNT, C), output_weight_matrix, precision=highest) + output_bias_vector
    return updated + gate * result.reshape(RESIDUE_COUNT, RESIDUE_COUNT, C)
```

```python
import functools

import jax
import jax.numpy as jnp
from jax import lax
from jax.experimental import pallas as pl
from jax.experimental.pallas import tpu as pltpu
from jax.sharding import PartitionSpec as P

SEQUENCE_COUNT = 128
EPSILON = 1e-05
LANES = 128
VMEM_LIMIT = 32 * 1024 * 1024


def split(value):
    high = value.astype(jnp.bfloat16)
    return high, (value - high.astype(jnp.float32)).astype(jnp.bfloat16)


def product(left, right, transposed):
    dims = (((1,), (1 if transposed else 0,)), ((), ()))
    dot = functools.partial(
        lax.dot_general, dimension_numbers=dims, preferred_element_type=jnp.float32
    )
    return dot(left[0], right[0]) + (dot(left[0], right[1]) + dot(left[1], right[0]))


def swap_groups(blocks):
    lane = lax.broadcasted_iota(jnp.int32, blocks[0].shape, 1)
    wide, narrow = (lane & 64) == 0, (lane & 32) == 0

    def exchange(first, second, shift, mask):
        return (
            jnp.where(mask, first, pltpu.roll(second, shift, 1)),
            jnp.where(mask, pltpu.roll(first, LANES - shift, 1), second),
        )

    a, c = exchange(blocks[0], blocks[2], 64, wide)
    b, d = exchange(blocks[1], blocks[3], 64, wide)
    a, b = exchange(a, b, 32, narrow)
    c, d = exchange(c, d, 32, narrow)
    return a, b, c, d


def tile_kernel(
    row_ref,
    own_ref,
    other_ref,
    right_ref,
    pair_ref,
    mean_weight_ref,
    mean_bias_ref,
    gain_ref,
    shift_ref,
    weight_ref,
    send_ref,
    updated_ref,
    gate_ref,
    right_scratch,
    high_scratch,
    low_scratch,
):
    row = row_ref[0]
    for step in range(8):
        place = pl.multiple_of((row ^ step) * 32, 32)
        right_scratch[pl.ds(place, 32), :] = right_ref[step]
    right = split(
        jnp.concatenate([right_scratch[pl.ds(j, 32, stride=8), :] for j in range(8)], axis=0)
    )
    own, other = own_ref[...], other_ref[...]
    first_half = lax.broadcasted_iota(jnp.int32, own.shape, 1) < 64
    halves = (
        jnp.where(first_half, own, pltpu.roll(other, 64, 1)),
        jnp.where(first_half, pltpu.roll(own, 64, 1), other),
    )
    for half in range(2):
        outer = product(split(halves[half]), right, True)
        for wide in range(2):
            for group in range(8):
                blocks = [
                    outer[
                        (group * 4 + p) * 16 : (group * 4 + p + 1) * 16,
                        wide * LANES : (wide + 1) * LANES,
                    ]
                    for p in range(4)
                ]
                for j, block in enumerate(swap_groups(blocks)):
                    rows = pl.ds((wide * 4 + j) * 32 + half * 16, 16)
                    columns = pl.ds(group * LANES, LANES)
                    high, low = split(block)
                    high_scratch[rows, columns] = high
                    low_scratch[rows, columns] = low
    summed = product(
        (high_scratch[...], low_scratch[...]), split(mean_weight_ref[...]), False
    )
    pair = jnp.concatenate([pair_ref[pl.ds(j, 32, stride=8), :] for j in range(8)], axis=0)
    updated = pair + (summed + mean_bias_ref[...]) * (1.0 / SEQUENCE_COUNT)
    updated_ref[...] = updated
    center = updated - jnp.mean(updated, axis=1, keepdims=True)
    spread = jnp.mean(center * center, axis=1, keepdims=True)
    normed = center * lax.rsqrt(spread + EPSILON) * gain_ref[...] + shift_ref[...]
    one = (lax.broadcasted_iota(jnp.int32, normed.shape, 1) == 0).astype(jnp.float32)
    proj = product(split(weight_ref[...]), split(jnp.concatenate([normed, one], axis=1)), True)
    blocks = [proj[n * LANES : (n + 1) * LANES] for n in range(5)]
    left_act = jax.nn.sigmoid(blocks[1]) * blocks[0]
    right_act = jax.nn.sigmoid(blocks[3]) * blocks[2]
    send_ref[pl.ds(0, 128, stride=4), :] = left_act[:, :LANES]
    send_ref[pl.ds(1, 128, stride=4), :] = left_act[:, LANES:]
    send_ref[pl.ds(2, 128, stride=4), :] = right_act[:, :LANES]
    send_ref[pl.ds(3, 128, stride=4), :] = right_act[:, LANES:]
    gate_ref[...] = jax.nn.sigmoid(blocks[4])


def triangle_kernel(core_ref, own_ref, other_ref, send_ref, left_scratch, right_scratch):
    first_core = core_ref[0] == 0

    def regroup(source, part, wide):
        return swap_groups([source(wide * 4 + r, part) for r in range(4)])

    def rows_of(ref):
        return lambda r, part: ref[pl.ds(r * 64 + part, 16, stride=4), :]

    own, other = rows_of(own_ref), rows_of(other_ref)

    def lower(r, part):
        return jnp.where(first_core, own(r, part), other(r, part))

    def upper(r, part):
        return jnp.where(first_core, other(r, part), own(r, part))

    for wide in range(2):
        for part in range(2):
            for core, source in enumerate((lower, upper)):
                for g, block in enumerate(regroup(source, part, wide)):
                    place = core * 8 + part * 4 + g
                    left_scratch[wide, pl.ds(place, 16, stride=16), :] = block
            for g, block in enumerate(regroup(own, part + 2, wide)):
                right_scratch[wide, pl.ds((part * 4 + g) * 16, 16), :] = block
    left = split(jnp.concatenate([left_scratch[0], left_scratch[1]], axis=1))
    right = split(jnp.concatenate([right_scratch[0], right_scratch[1]], axis=1))
    mixed = product(right, left, True)
    for wide in range(2):
        for part in range(2):
            blocks = [
                mixed[
                    (part * 4 + g) * 16 : (part * 4 + g + 1) * 16,
                    wide * LANES : (wide + 1) * LANES,
                ]
                for g in range(4)
            ]
            for r, block in enumerate(swap_groups(blocks)):
                send_ref[pl.ds((wide * 4 + r) * 32 + part, 16, stride=2), :] = block


def output_kernel(mixed_ref, updated_ref, gate_ref, gain_ref, shift_ref, weight_ref, out_ref):
    mixed = jnp.concatenate(
        [mixed_ref[pl.ds(0, 128, stride=2), :], mixed_ref[pl.ds(1, 128, stride=2), :]], axis=1
    )
    center = mixed - jnp.mean(mixed, axis=0, keepdims=True)
    spread = jnp.mean(center * center, axis=0, keepdims=True)
    normed = center * lax.rsqrt(spread + EPSILON)
    weight = weight_ref[:, :LANES]
    bias = jnp.sum(weight * shift_ref[...], axis=1, keepdims=True) + weight_ref[:, LANES : LANES + 1]
    result = product(split(weight * gain_ref[...]), split(normed), False) + bias
    gated = jnp.transpose(gate_ref[...] * result)
    out = updated_ref[...] + gated
    for j in range(8):
        out_ref[pl.ds(j, 32, stride=8), :] = out[j * 32 : (j + 1) * 32]


def call(kernel, outputs, scratch, scalars, *operands):
    specs = [pl.BlockSpec(memory_space=pltpu.SMEM)] * scalars
    specs += [pl.BlockSpec(memory_space=pltpu.VMEM)] * (len(operands) - scalars)
    return pl.pallas_call(
        kernel,
        out_shape=[jax.ShapeDtypeStruct(shape, jnp.float32) for shape in outputs],
        in_specs=specs,
        out_specs=[pl.BlockSpec(memory_space=pltpu.VMEM)] * len(outputs),
        scratch_shapes=scratch,
        compiler_params=pltpu.CompilerParams(vmem_limit_bytes=VMEM_LIMIT),
    )(*operands)


def exchange(value, axis, distance):
    count = lax.axis_size(axis)
    return lax.ppermute(value, axis, [(n, n ^ distance) for n in range(count)])


def with_bias(weight, bias):
    rows = jnp.zeros((LANES, weight.shape[1]), jnp.float32).at[0].set(bias)
    return jnp.concatenate([weight, rows], axis=0).T


def per_device(
    pair,
    alignment_left,
    alignment_right,
    outer_mean_weight,
    outer_mean_bias,
    input_norm_gain,
    input_norm_bias,
    input_weight_matrix,
    input_bias_vector,
    output_norm_gain,
    output_norm_bias,
    output_weight_matrix,
    output_bias_vector,
):
    row, core = lax.axis_index("row"), lax.axis_index("seq")
    columns = alignment_right.transpose(2, 1, 0)
    mine = lax.dynamic_slice_in_dim(columns, core * 8, 8, 1)
    theirs = lax.dynamic_slice_in_dim(columns, (1 - core) * 8, 8, 1)
    right = jnp.concatenate([mine, exchange(theirs, "seq", 1)], axis=2).reshape(1, 32, LANES)
    for distance in (1, 2, 4):
        right = jnp.concatenate([right, exchange(right, "row", distance)], axis=0)
    left = alignment_left.transpose(2, 1, 0).reshape(2, 2, 16, 64)
    left = left.transpose(0, 2, 1, 3).reshape(1, 32, LANES)
    left = jnp.broadcast_to(left, (16, 32, LANES)).reshape(512, LANES)
    own = lax.all_to_all(left, "col", 0, 0, tiled=True)
    other = exchange(own, "seq", 1)
    send, updated, gate = call(
        tile_kernel,
        [(512, LANES), (256, LANES), (LANES, 256)],
        [
            pltpu.VMEM((256, LANES), jnp.float32),
            pltpu.VMEM((256, 1024), jnp.bfloat16),
            pltpu.VMEM((256, 1024), jnp.bfloat16),
        ],
        1,
        row.reshape(1),
        own,
        other,
        right,
        pair.reshape(256, LANES),
        outer_mean_weight,
        outer_mean_bias.reshape(1, LANES),
        input_norm_gain.reshape(1, LANES),
        input_norm_bias.reshape(1, LANES),
        with_bias(input_weight_matrix, input_bias_vector),
    )
    own = lax.all_to_all(send, ("row", "col"), 0, 0, tiled=True)
    other = exchange(own, "seq", 1)
    (back,) = call(
        triangle_kernel,
        [(256, LANES)],
        [
            pltpu.VMEM((2, 256, LANES), jnp.float32),
            pltpu.VMEM((2, 128, LANES), jnp.float32),
        ],
        1,
        core.reshape(1),
        own,
        other,
    )
    mixed = lax.all_to_all(back, ("row", "col"), 0, 0, tiled=True)
    (out,) = call(
        output_kernel,
        [(256, LANES)],
        [],
        0,
        mixed,
        updated,
        gate,
        output_norm_gain.reshape(1, LANES),
        output_norm_bias.reshape(1, LANES),
        with_bias(output_weight_matrix, output_bias_vector),
    )
    return out.reshape(pair.shape)


def solution(mesh):
    return jax.shard_map(
        per_device,
        mesh=mesh,
        in_specs=(
            P("row", ("col", "seq"), None),
            P("seq", "row", "col"),
            P("seq", "col", "row"),
            P(),
            P(),
            P(),
            P(),
            P(),
            P(),
            P(),
            P(),
            P(),
            P(),
        ),
        out_specs=P("row", ("col", "seq"), None),
        check_vma=False,
    )
```

```python
import functools

import jax
import jax.numpy as jnp
from jax import lax
from jax.experimental import pallas as pl
from jax.experimental.pallas import tpu as pltpu
from jax.sharding import PartitionSpec as P

SEQUENCE_COUNT = 128
EPSILON = 1e-05
LANES = 128
VMEM_LIMIT = 32 * 1024 * 1024


def split(value):
    high = value.astype(jnp.bfloat16)
    return high, (value - high.astype(jnp.float32)).astype(jnp.bfloat16)


def product(left, right, transposed):
    dims = (((1,), (1 if transposed else 0,)), ((), ()))
    dot = functools.partial(
        lax.dot_general, dimension_numbers=dims, preferred_element_type=jnp.float32
    )
    return dot(left[0], right[0]) + (dot(left[0], right[1]) + dot(left[1], right[0]))


def swap_groups(blocks):
    lane = lax.broadcasted_iota(jnp.int32, blocks[0].shape, 1)
    wide, narrow = (lane & 64) == 0, (lane & 32) == 0

    def exchange(first, second, shift, mask):
        return (
            jnp.where(mask, first, pltpu.roll(second, shift, 1)),
            jnp.where(mask, pltpu.roll(first, LANES - shift, 1), second),
        )

    a, c = exchange(blocks[0], blocks[2], 64, wide)
    b, d = exchange(blocks[1], blocks[3], 64, wide)
    a, b = exchange(a, b, 32, narrow)
    c, d = exchange(c, d, 32, narrow)
    return a, b, c, d


def pack_kernel(core_ref, kept_ref, got_ref, vectors_ref, out_ref, vectors_out_ref):
    vectors_out_ref[...] = vectors_ref[...]
    first_core = core_ref[0] == 0

    def ordered(ref):
        left = [ref[pl.ds(p, 32, stride=2), :] for p in range(2)]
        right = [ref[pl.ds(q, 16, stride=4), :] for q in range(4)]
        return jnp.where(first_core, jnp.concatenate(left, axis=0), jnp.concatenate(right, axis=0))

    kept, got = ordered(kept_ref), ordered(got_ref)
    lower, upper = jnp.where(first_core, kept, got), jnp.where(first_core, got, kept)
    block = jnp.concatenate([lower, upper], axis=1)
    for n in range(16):
        out_ref[pl.ds(n * 64, 64), :] = block


def tile_kernel(
    place_ref,
    own_ref,
    other_ref,
    pair_ref,
    mean_weight_ref,
    weight_ref,
    vectors_ref,
    send_ref,
    updated_ref,
    gate_ref,
    right_scratch,
    high_scratch,
    low_scratch,
):
    core, odd = place_ref[0], place_ref[1]
    first_core = core == 0
    for row in range(8):
        for q in range(4):
            start = odd * 512 + row * 64 + q * 16 + core * 8
            rows = pl.ds(pl.multiple_of(start, 8), 8)
            right_scratch[pl.ds(row * 32 + q * 8, 8), :] = jnp.where(
                first_core, other_ref[rows, :], own_ref[rows, :]
            )
    right = split(
        jnp.concatenate([right_scratch[pl.ds(j, 32, stride=8), :] for j in range(8)], axis=0)
    )
    left = jnp.where(first_core, own_ref[...], other_ref[...])
    outer = product(split(left), right, True)
    for wide in range(2):
        for group in range(8):
            blocks = [
                outer[
                    (group * 4 + p) * 32 : (group * 4 + p + 1) * 32,
                    wide * LANES : (wide + 1) * LANES,
                ]
                for p in range(4)
            ]
            for j, block in enumerate(swap_groups(blocks)):
                rows = pl.ds((wide * 4 + j) * 32, 32)
                columns = pl.ds(group * LANES, LANES)
                high, low = split(block)
                high_scratch[rows, columns] = high
                low_scratch[rows, columns] = low
    summed = product(
        (high_scratch[...], low_scratch[...]), split(mean_weight_ref[...]), False
    )
    pair = jnp.concatenate([pair_ref[pl.ds(j, 32, stride=8), :] for j in range(8)], axis=0)
    updated = pair + (summed + vectors_ref[0:1]) * (1.0 / SEQUENCE_COUNT)
    updated_ref[...] = updated
    center = updated - jnp.mean(updated, axis=1, keepdims=True)
    spread = jnp.mean(center * center, axis=1, keepdims=True)
    normed = center * lax.rsqrt(spread + EPSILON) * vectors_ref[1:2] + vectors_ref[2:3]
    proj = product(split(normed), split(weight_ref[...]), False)
    blocks = [
        proj[:, n * LANES : (n + 1) * LANES] + vectors_ref[6 + n : 7 + n] for n in range(5)
    ]
    left_act = jnp.transpose(jax.nn.sigmoid(blocks[1]) * blocks[0])
    right_act = jnp.transpose(jax.nn.sigmoid(blocks[3]) * blocks[2])
    send_ref[pl.ds(0, 128, stride=4), :] = left_act[:, :LANES]
    send_ref[pl.ds(1, 128, stride=4), :] = left_act[:, LANES:]
    send_ref[pl.ds(2, 128, stride=4), :] = right_act[:, :LANES]
    send_ref[pl.ds(3, 128, stride=4), :] = right_act[:, LANES:]
    gate_ref[...] = jax.nn.sigmoid(blocks[4])


def triangle_kernel(core_ref, own_ref, other_ref, send_ref, left_scratch, right_scratch):
    first_core = core_ref[0] == 0

    def regroup(source, part, wide):
        return swap_groups([source(wide * 4 + r, part) for r in range(4)])

    def rows_of(ref):
        return lambda r, part: ref[pl.ds(r * 64 + part, 16, stride=4), :]

    own, other = rows_of(own_ref), rows_of(other_ref)

    def lower(r, part):
        return jnp.where(first_core, own(r, part), other(r, part))

    def upper(r, part):
        return jnp.where(first_core, other(r, part), own(r, part))

    for wide in range(2):
        for part in range(2):
            for core, source in enumerate((lower, upper)):
                for g, block in enumerate(regroup(source, part, wide)):
                    place = core * 8 + part * 4 + g
                    left_scratch[wide, pl.ds(place, 16, stride=16), :] = block
            for g, block in enumerate(regroup(own, part + 2, wide)):
                right_scratch[wide, pl.ds((part * 4 + g) * 16, 16), :] = block
    left = split(jnp.concatenate([left_scratch[0], left_scratch[1]], axis=1))
    right = split(jnp.concatenate([right_scratch[0], right_scratch[1]], axis=1))
    mixed = product(right, left, True)
    for wide in range(2):
        for part in range(2):
            blocks = [
                mixed[
                    (part * 4 + g) * 16 : (part * 4 + g + 1) * 16,
                    wide * LANES : (wide + 1) * LANES,
                ]
                for g in range(4)
            ]
            for r, block in enumerate(swap_groups(blocks)):
                send_ref[pl.ds((wide * 4 + r) * 32 + part, 16, stride=2), :] = block


def output_kernel(mixed_ref, updated_ref, gate_ref, weight_ref, vectors_ref, out_ref):
    mixed = jnp.concatenate(
        [mixed_ref[pl.ds(0, 128, stride=2), :], mixed_ref[pl.ds(1, 128, stride=2), :]], axis=1
    )
    center = mixed - jnp.mean(mixed, axis=0, keepdims=True)
    spread = jnp.mean(center * center, axis=0, keepdims=True)
    normed = jnp.transpose(center * lax.rsqrt(spread + EPSILON))
    normed = normed * vectors_ref[3:4] + vectors_ref[4:5]
    result = product(split(normed), split(weight_ref[...]), False) + vectors_ref[5:6]
    out = updated_ref[...] + gate_ref[...] * result
    for j in range(8):
        out_ref[pl.ds(j, 32, stride=8), :] = out[j * 32 : (j + 1) * 32]


def call(kernel, outputs, scratch, scalars, *blocks):
    specs = [pl.BlockSpec(memory_space=pltpu.SMEM)] * len(scalars)
    specs += [pl.BlockSpec(memory_space=pltpu.VMEM)] * len(blocks)
    return pl.pallas_call(
        kernel,
        out_shape=[jax.ShapeDtypeStruct(shape, jnp.float32) for shape in outputs],
        in_specs=specs,
        out_specs=[pl.BlockSpec(memory_space=pltpu.VMEM)] * len(outputs),
        scratch_shapes=scratch,
        compiler_params=pltpu.CompilerParams(vmem_limit_bytes=VMEM_LIMIT),
    )(*scalars, *blocks)


def exchange(value, axis, distance):
    count = lax.axis_size(axis)
    return lax.ppermute(value, axis, [(n, n ^ distance) for n in range(count)])


def gather_groups(rows, columns):
    place = lambda row, column, core: (row * columns + column) * 2 + core
    first = [[place(row, column, 0) for column in range(columns)] for row in range(rows)]
    second = [
        [place(row, column + n, 1) for n in range(2) for row in range(rows)]
        for column in range(0, columns, 2)
    ]
    return first + second


def per_device(
    pair,
    alignment_left,
    alignment_right,
    outer_mean_weight,
    outer_mean_bias,
    input_norm_gain,
    input_norm_bias,
    input_weight_matrix,
    input_bias_vector,
    output_norm_gain,
    output_norm_bias,
    output_weight_matrix,
    output_bias_vector,
):
    core = lax.axis_index("seq")
    place = jnp.stack([core, lax.axis_index("col") % 2])
    core_array = core.reshape(1)
    left = alignment_left.transpose(1, 2, 0).reshape(64, 64)
    right = alignment_right.transpose(1, 2, 0).reshape(64, 64)
    kept = jnp.where(core == 0, left, right)
    got = exchange(jnp.where(core == 0, right, left), "seq", 1)
    vectors = [
        outer_mean_bias,
        input_norm_gain,
        input_norm_bias,
        output_norm_gain,
        output_norm_bias,
        output_bias_vector,
        input_bias_vector,
    ]
    vectors = jnp.concatenate([vector.reshape(-1, LANES) for vector in vectors], axis=0)
    blocks, vectors = call(
        pack_kernel,
        [(1024, LANES), vectors.shape],
        [],
        [core_array],
        kept,
        got,
        vectors,
    )
    own = lax.all_to_all(
        blocks,
        ("row", "col", "seq"),
        0,
        0,
        tiled=True,
        axis_index_groups=gather_groups(lax.axis_size("row"), lax.axis_size("col")),
    )
    send, updated, gate = call(
        tile_kernel,
        [(512, LANES), (256, LANES), (256, LANES)],
        [
            pltpu.VMEM((256, LANES), jnp.float32),
            pltpu.VMEM((256, 1024), jnp.bfloat16),
            pltpu.VMEM((256, 1024), jnp.bfloat16),
        ],
        [place],
        own,
        exchange(own, "seq", 1),
        pair.reshape(256, LANES),
        outer_mean_weight,
        input_weight_matrix,
        vectors,
    )
    own = lax.all_to_all(send, ("row", "col"), 0, 0, tiled=True)
    (back,) = call(
        triangle_kernel,
        [(256, LANES)],
        [
            pltpu.VMEM((2, 256, LANES), jnp.float32),
            pltpu.VMEM((2, 128, LANES), jnp.float32),
        ],
        [core_array],
        own,
        exchange(own, "seq", 1),
    )
    mixed = lax.all_to_all(back, ("row", "col"), 0, 0, tiled=True)
    (out,) = call(
        output_kernel,
        [(256, LANES)],
        [],
        [],
        mixed,
        updated,
        gate,
        output_weight_matrix,
        vectors,
    )
    return out.reshape(pair.shape)


def solution(mesh):
    return jax.shard_map(
        per_device,
        mesh=mesh,
        in_specs=(
            P("row", ("col", "seq"), None),
            P("seq", "row", "col"),
            P("seq", "col", "row"),
            P(),
            P(),
            P(),
            P(),
            P(),
            P(),
            P(),
            P(),
            P(),
            P(),
        ),
        out_specs=P("row", ("col", "seq"), None),
        check_vma=False,
    )
```

```python
import functools

import jax
import jax.numpy as jnp
from jax import lax
from jax.experimental import pallas as pl
from jax.experimental.pallas import tpu as pltpu
from jax.sharding import PartitionSpec as P

SEQUENCE_COUNT = 128
EPSILON = 1e-05
LANES = 128
VMEM_LIMIT = 32 * 1024 * 1024
FAR_ROW, FAR_COLUMN = 4, 10


def split(value):
    high = value.astype(jnp.bfloat16)
    return high, (value - high.astype(jnp.float32)).astype(jnp.bfloat16)


def product(left, right, transposed):
    dims = (((1,), (1 if transposed else 0,)), ((), ()))
    dot = functools.partial(
        lax.dot_general, dimension_numbers=dims, preferred_element_type=jnp.float32
    )
    return dot(left[0], right[0]) + (dot(left[0], right[1]) + dot(left[1], right[0]))


def swap_groups(blocks):
    lane = lax.broadcasted_iota(jnp.int32, blocks[0].shape, 1)
    wide, narrow = (lane & 64) == 0, (lane & 32) == 0

    def exchange(first, second, shift, mask):
        return (
            jnp.where(mask, first, pltpu.roll(second, shift, 1)),
            jnp.where(mask, pltpu.roll(first, LANES - shift, 1), second),
        )

    a, c = exchange(blocks[0], blocks[2], 64, wide)
    b, d = exchange(blocks[1], blocks[3], 64, wide)
    a, b = exchange(a, b, 32, narrow)
    c, d = exchange(c, d, 32, narrow)
    return a, b, c, d


def pack_kernel(core_ref, kept_ref, got_ref, vectors_ref, out_ref, vectors_out_ref):
    vectors_out_ref[...] = vectors_ref[...]
    first_core = core_ref[0] == 0

    def ordered(ref):
        left = [ref[pl.ds(p, 32, stride=2), :] for p in range(2)]
        right = [ref[pl.ds(q, 16, stride=4), :] for q in range(4)]
        return jnp.where(first_core, jnp.concatenate(left, axis=0), jnp.concatenate(right, axis=0))

    kept, got = ordered(kept_ref), ordered(got_ref)
    lower, upper = jnp.where(first_core, kept, got), jnp.where(first_core, got, kept)
    block = jnp.concatenate([lower, upper], axis=1)
    for n in range(16):
        out_ref[pl.ds(n * 64, 64), :] = block


def tile_kernel(
    place_ref,
    own_ref,
    other_ref,
    pair_ref,
    mean_weight_ref,
    weight_ref,
    vectors_ref,
    send_ref,
    updated_ref,
    gate_ref,
    right_scratch,
    high_scratch,
    low_scratch,
):
    core, odd = place_ref[0], place_ref[1]
    first_core = core == 0
    for row in range(8):
        for q in range(4):
            start = odd * 512 + row * 64 + q * 16 + core * 8
            rows = pl.ds(pl.multiple_of(start, 8), 8)
            right_scratch[pl.ds((row ^ FAR_ROW) * 32 + q * 8, 8), :] = jnp.where(
                first_core, other_ref[rows, :], own_ref[rows, :]
            )
    right = split(
        jnp.concatenate([right_scratch[pl.ds(j, 32, stride=8), :] for j in range(8)], axis=0)
    )
    left = jnp.where(first_core, own_ref[...], other_ref[...])
    outer = product(split(left), right, True)
    for wide in range(2):
        for group in range(8):
            blocks = [
                outer[
                    (group * 4 + p) * 32 : (group * 4 + p + 1) * 32,
                    wide * LANES : (wide + 1) * LANES,
                ]
                for p in range(4)
            ]
            for j, block in enumerate(swap_groups(blocks)):
                rows = pl.ds((wide * 4 + j) * 32, 32)
                columns = pl.ds((group ^ (FAR_COLUMN // 2)) * LANES, LANES)
                high, low = split(block)
                high_scratch[rows, columns] = high
                low_scratch[rows, columns] = low
    summed = product(
        (high_scratch[...], low_scratch[...]), split(mean_weight_ref[...]), False
    )
    pair = jnp.concatenate([pair_ref[pl.ds(j, 32, stride=8), :] for j in range(8)], axis=0)
    updated = pair + (summed + vectors_ref[0:1]) * (1.0 / SEQUENCE_COUNT)
    updated_ref[...] = updated
    center = updated - jnp.mean(updated, axis=1, keepdims=True)
    spread = jnp.mean(center * center, axis=1, keepdims=True)
    normed = center * lax.rsqrt(spread + EPSILON) * vectors_ref[1:2] + vectors_ref[2:3]
    proj = product(split(normed), split(weight_ref[...]), False)
    blocks = [
        proj[:, n * LANES : (n + 1) * LANES] + vectors_ref[6 + n : 7 + n] for n in range(5)
    ]
    left_act = jnp.transpose(jax.nn.sigmoid(blocks[1]) * blocks[0])
    right_act = jnp.transpose(jax.nn.sigmoid(blocks[3]) * blocks[2])
    send_ref[pl.ds(0, 128, stride=4), :] = left_act[:, :LANES]
    send_ref[pl.ds(1, 128, stride=4), :] = left_act[:, LANES:]
    send_ref[pl.ds(2, 128, stride=4), :] = right_act[:, :LANES]
    send_ref[pl.ds(3, 128, stride=4), :] = right_act[:, LANES:]
    gate_ref[...] = jax.nn.sigmoid(blocks[4])


def triangle_kernel(core_ref, own_ref, other_ref, send_ref, left_scratch, right_scratch):
    first_core = core_ref[0] == 0

    def regroup(source, part, wide):
        return swap_groups([source(wide * 4 + r, part) for r in range(4)])

    def rows_of(ref):
        return lambda r, part: ref[pl.ds(r * 64 + part, 16, stride=4), :]

    own, other = rows_of(own_ref), rows_of(other_ref)

    def lower(r, part):
        return jnp.where(first_core, own(r, part), other(r, part))

    def upper(r, part):
        return jnp.where(first_core, other(r, part), own(r, part))

    for wide in range(2):
        for part in range(2):
            for core, source in enumerate((lower, upper)):
                for g, block in enumerate(regroup(source, part, wide)):
                    place = core * 8 + part * 4 + g
                    left_scratch[wide, pl.ds(place, 16, stride=16), :] = block
            for g, block in enumerate(regroup(own, part + 2, wide)):
                right_scratch[wide, pl.ds((part * 4 + g) * 16, 16), :] = block
    left = split(jnp.concatenate([left_scratch[0], left_scratch[1]], axis=1))
    right = split(jnp.concatenate([right_scratch[0], right_scratch[1]], axis=1))
    mixed = product(right, left, True)
    for wide in range(2):
        for part in range(2):
            blocks = [
                mixed[
                    (part * 4 + g) * 16 : (part * 4 + g + 1) * 16,
                    wide * LANES : (wide + 1) * LANES,
                ]
                for g in range(4)
            ]
            for r, block in enumerate(swap_groups(blocks)):
                place = (wide * 4 + r) ^ (FAR_COLUMN // 2) ^ FAR_ROW
                send_ref[pl.ds(place * 32 + part, 16, stride=2), :] = block


def output_kernel(mixed_ref, updated_ref, gate_ref, weight_ref, vectors_ref, out_ref):
    mixed = jnp.concatenate(
        [mixed_ref[pl.ds(0, 128, stride=2), :], mixed_ref[pl.ds(1, 128, stride=2), :]], axis=1
    )
    center = mixed - jnp.mean(mixed, axis=0, keepdims=True)
    spread = jnp.mean(center * center, axis=0, keepdims=True)
    normed = jnp.transpose(center * lax.rsqrt(spread + EPSILON))
    normed = normed * vectors_ref[3:4] + vectors_ref[4:5]
    result = product(split(normed), split(weight_ref[...]), False) + vectors_ref[5:6]
    out = updated_ref[...] + gate_ref[...] * result
    for j in range(8):
        out_ref[pl.ds(j, 32, stride=8), :] = out[j * 32 : (j + 1) * 32]


def call(kernel, outputs, scratch, scalars, *blocks):
    specs = [pl.BlockSpec(memory_space=pltpu.SMEM)] * len(scalars)
    specs += [pl.BlockSpec(memory_space=pltpu.VMEM)] * len(blocks)
    return pl.pallas_call(
        kernel,
        out_shape=[jax.ShapeDtypeStruct(shape, jnp.float32) for shape in outputs],
        in_specs=specs,
        out_specs=[pl.BlockSpec(memory_space=pltpu.VMEM)] * len(outputs),
        scratch_shapes=scratch,
        compiler_params=pltpu.CompilerParams(vmem_limit_bytes=VMEM_LIMIT),
    )(*scalars, *blocks)


def exchange(value, axis, distance):
    count = lax.axis_size(axis)
    return lax.ppermute(value, axis, [(n, n ^ distance) for n in range(count)])


def far_first(rows, columns):
    return [(row ^ FAR_ROW, column ^ FAR_COLUMN) for row in range(rows) for column in range(columns)]


def exchange_groups(rows, columns):
    places = far_first(rows, columns)
    return [[(row * columns + column) * 2 + core for row, column in places] for core in range(2)]


def gather_groups(rows, columns):
    place = lambda row, column, core: (row * columns + column) * 2 + core
    first = [
        [place(row, column ^ FAR_COLUMN, 0) for column in range(columns)] for row in range(rows)
    ]
    second = [
        [place(row ^ FAR_ROW, column + n, 1) for n in range(2) for row in range(rows)]
        for column in range(0, columns, 2)
    ]
    return first + second


def per_device(
    pair,
    alignment_left,
    alignment_right,
    outer_mean_weight,
    outer_mean_bias,
    input_norm_gain,
    input_norm_bias,
    input_weight_matrix,
    input_bias_vector,
    output_norm_gain,
    output_norm_bias,
    output_weight_matrix,
    output_bias_vector,
):
    rows, columns = lax.axis_size("row"), lax.axis_size("col")

    def spread(value, groups):
        return lax.all_to_all(
            value, ("row", "col", "seq"), 0, 0, tiled=True, axis_index_groups=groups
        )

    core = lax.axis_index("seq")
    place = jnp.stack([core, lax.axis_index("col") % 2])
    core_array = core.reshape(1)
    left = alignment_left.transpose(1, 2, 0).reshape(64, 64)
    right = alignment_right.transpose(1, 2, 0).reshape(64, 64)
    kept = jnp.where(core == 0, left, right)
    got = exchange(jnp.where(core == 0, right, left), "seq", 1)
    vectors = [
        outer_mean_bias,
        input_norm_gain,
        input_norm_bias,
        output_norm_gain,
        output_norm_bias,
        output_bias_vector,
        input_bias_vector,
    ]
    vectors = jnp.concatenate([vector.reshape(-1, LANES) for vector in vectors], axis=0)
    blocks, vectors = call(
        pack_kernel,
        [(1024, LANES), vectors.shape],
        [],
        [core_array],
        kept,
        got,
        vectors,
    )
    own = spread(blocks, gather_groups(rows, columns))
    send, updated, gate = call(
        tile_kernel,
        [(512, LANES), (256, LANES), (256, LANES)],
        [
            pltpu.VMEM((256, LANES), jnp.float32),
            pltpu.VMEM((256, 1024), jnp.bfloat16),
            pltpu.VMEM((256, 1024), jnp.bfloat16),
        ],
        [place],
        own,
        exchange(own, "seq", 1),
        pair.reshape(256, LANES),
        outer_mean_weight,
        input_weight_matrix,
        vectors,
    )
    own = spread(send, exchange_groups(rows, columns))
    (back,) = call(
        triangle_kernel,
        [(256, LANES)],
        [
            pltpu.VMEM((2, 256, LANES), jnp.float32),
            pltpu.VMEM((2, 128, LANES), jnp.float32),
        ],
        [core_array],
        own,
        exchange(own, "seq", 1),
    )
    mixed = spread(back, exchange_groups(rows, columns))
    (out,) = call(
        output_kernel,
        [(256, LANES)],
        [],
        [],
        mixed,
        updated,
        gate,
        output_weight_matrix,
        vectors,
    )
    return out.reshape(pair.shape)


def solution(mesh):
    return jax.shard_map(
        per_device,
        mesh=mesh,
        in_specs=(
            P("row", ("col", "seq"), None),
            P("seq", "row", "col"),
            P("seq", "col", "row"),
            P(),
            P(),
            P(),
            P(),
            P(),
            P(),
            P(),
            P(),
            P(),
            P(),
        ),
        out_specs=P("row", ("col", "seq"), None),
        check_vma=False,
    )
```

```python
import functools

import jax
import jax.numpy as jnp
from jax import lax
from jax.experimental import pallas as pl
from jax.experimental.pallas import tpu as pltpu
from jax.sharding import PartitionSpec as P

SEQUENCE_COUNT = 128
EPSILON = 1e-05
LANES = 128
VMEM_LIMIT = 32 * 1024 * 1024
FAR_ROW, FAR_COLUMN = 4, 10


def split(value):
    high = value.astype(jnp.bfloat16)
    return high, (value - high.astype(jnp.float32)).astype(jnp.bfloat16)


def product(left, right, transposed):
    dims = (((1,), (1 if transposed else 0,)), ((), ()))
    dot = functools.partial(
        lax.dot_general, dimension_numbers=dims, preferred_element_type=jnp.float32
    )
    if left[0].shape[1] == LANES:
        return dot(
            jnp.concatenate([left[0], left[1], left[0]], axis=1),
            jnp.concatenate([right[0], right[0], right[1]], axis=1 if transposed else 0),
        )
    if right[0].shape[1] == LANES and not transposed:
        both = dot(left[0], jnp.concatenate([right[0], right[1]], axis=1))
        return both[:, :LANES] + (both[:, LANES:] + dot(left[1], right[0]))
    return dot(left[0], right[0]) + (dot(left[0], right[1]) + dot(left[1], right[0]))


def swap_groups(blocks):
    lane = lax.broadcasted_iota(jnp.int32, blocks[0].shape, 1)
    wide, narrow = (lane & 64) == 0, (lane & 32) == 0

    def exchange(first, second, shift, mask):
        return (
            jnp.where(mask, first, pltpu.roll(second, shift, 1)),
            jnp.where(mask, pltpu.roll(first, LANES - shift, 1), second),
        )

    a, c = exchange(blocks[0], blocks[2], 64, wide)
    b, d = exchange(blocks[1], blocks[3], 64, wide)
    a, b = exchange(a, b, 32, narrow)
    c, d = exchange(c, d, 32, narrow)
    return a, b, c, d


def pack_kernel(core_ref, kept_ref, left_ref, right_ref, out_ref):
    first_core = core_ref[0] == 0

    def ordered(left_ref, right_ref):
        left = [left_ref[pl.ds(p, 32, stride=2), :] for p in range(2)]
        right = [right_ref[pl.ds(q, 16, stride=4), :] for q in range(4)]
        return jnp.where(first_core, jnp.concatenate(left, axis=0), jnp.concatenate(right, axis=0))

    kept, got = ordered(kept_ref, kept_ref), ordered(left_ref, right_ref)
    lower, upper = jnp.where(first_core, kept, got), jnp.where(first_core, got, kept)
    block = jnp.concatenate([lower, upper], axis=1)
    for n in range(16):
        out_ref[pl.ds(n * 64, 64), :] = block


def tile_kernel(
    place_ref,
    own_ref,
    other_ref,
    pair_ref,
    mean_weight_ref,
    weight_ref,
    vectors_ref,
    send_ref,
    updated_ref,
    gate_ref,
    right_scratch,
    high_scratch,
    low_scratch,
):
    core, odd = place_ref[0], place_ref[1]
    first_core = core == 0
    for row in range(8):
        for q in range(4):
            start = odd * 512 + row * 64 + q * 16 + core * 8
            rows = pl.ds(pl.multiple_of(start, 8), 8)
            right_scratch[pl.ds((row ^ FAR_ROW) * 32 + q * 8, 8), :] = jnp.where(
                first_core, other_ref[rows, :], own_ref[rows, :]
            )
    right = split(
        jnp.concatenate([right_scratch[pl.ds(j, 32, stride=8), :] for j in range(8)], axis=0)
    )
    left = jnp.where(first_core, own_ref[...], other_ref[...])
    outer = [product(split(left[n * 512 : (n + 1) * 512]), right, True) for n in range(2)]
    for group in range(8):
        for wide in range(2):
            blocks = [
                outer[group // 4][
                    (group % 4 * 4 + p) * 32 : (group % 4 * 4 + p + 1) * 32,
                    wide * LANES : (wide + 1) * LANES,
                ]
                for p in range(4)
            ]
            for j, block in enumerate(swap_groups(blocks)):
                rows = pl.ds((wide * 4 + j) * 32, 32)
                columns = pl.ds((group ^ (FAR_COLUMN // 2)) * LANES, LANES)
                high, low = split(block)
                high_scratch[rows, columns] = high
                low_scratch[rows, columns] = low
    summed = product(
        (high_scratch[...], low_scratch[...]), split(mean_weight_ref[...]), False
    )
    pair = jnp.concatenate([pair_ref[pl.ds(j, 32, stride=8), :] for j in range(8)], axis=0)
    updated = pair + (summed + vectors_ref[0:1]) * (1.0 / SEQUENCE_COUNT)
    updated_ref[...] = updated
    center = updated - jnp.mean(updated, axis=1, keepdims=True)
    spread = jnp.mean(center * center, axis=1, keepdims=True)
    normed = center * lax.rsqrt(spread + EPSILON) * vectors_ref[1:2] + vectors_ref[2:3]
    proj = product(split(normed), split(weight_ref[...]), False)
    blocks = [
        proj[:, n * LANES : (n + 1) * LANES] + vectors_ref[6 + n : 7 + n] for n in range(5)
    ]
    left_act = jnp.transpose(jax.nn.sigmoid(blocks[1]) * blocks[0])
    right_act = jnp.transpose(jax.nn.sigmoid(blocks[3]) * blocks[2])
    send_ref[pl.ds(0, 128, stride=4), :] = left_act[:, :LANES]
    send_ref[pl.ds(1, 128, stride=4), :] = left_act[:, LANES:]
    send_ref[pl.ds(2, 128, stride=4), :] = right_act[:, :LANES]
    send_ref[pl.ds(3, 128, stride=4), :] = right_act[:, LANES:]
    gate_ref[...] = jax.nn.sigmoid(blocks[4])


def triangle_kernel(core_ref, own_ref, other_ref, send_ref, left_scratch, right_scratch):
    first_core = core_ref[0] == 0

    def regroup(source, part, wide):
        return swap_groups([source(wide * 4 + r, part) for r in range(4)])

    def rows_of(ref):
        return lambda r, part: ref[pl.ds(r * 64 + part, 16, stride=4), :]

    own, other = rows_of(own_ref), rows_of(other_ref)

    def lower(r, part):
        return jnp.where(first_core, own(r, part), other(r, part))

    def upper(r, part):
        return jnp.where(first_core, other(r, part), own(r, part))

    for wide in range(2):
        for part in range(2):
            for core, source in enumerate((lower, upper)):
                for g, block in enumerate(regroup(source, part, wide)):
                    place = core * 8 + part * 4 + g
                    left_scratch[wide, pl.ds(place, 16, stride=16), :] = block
            for g, block in enumerate(regroup(own, part + 2, wide)):
                right_scratch[wide, pl.ds((part * 4 + g) * 16, 16), :] = block
    left = split(jnp.concatenate([left_scratch[0], left_scratch[1]], axis=1))
    right = split(jnp.concatenate([right_scratch[0], right_scratch[1]], axis=1))
    mixed = product(right, left, True)
    for wide in range(2):
        for part in range(2):
            blocks = [
                mixed[
                    (part * 4 + g) * 16 : (part * 4 + g + 1) * 16,
                    wide * LANES : (wide + 1) * LANES,
                ]
                for g in range(4)
            ]
            for r, block in enumerate(swap_groups(blocks)):
                place = (wide * 4 + r) ^ (FAR_COLUMN // 2) ^ FAR_ROW
                send_ref[pl.ds(place * 32 + part, 16, stride=2), :] = block


def output_kernel(mixed_ref, updated_ref, gate_ref, weight_ref, vectors_ref, out_ref):
    mixed = jnp.concatenate(
        [mixed_ref[pl.ds(0, 128, stride=2), :], mixed_ref[pl.ds(1, 128, stride=2), :]], axis=1
    )
    center = mixed - jnp.mean(mixed, axis=0, keepdims=True)
    spread = jnp.mean(center * center, axis=0, keepdims=True)
    normed = jnp.transpose(center * lax.rsqrt(spread + EPSILON))
    normed = normed * vectors_ref[3:4] + vectors_ref[4:5]
    result = product(split(normed), split(weight_ref[...]), False) + vectors_ref[5:6]
    out = updated_ref[...] + gate_ref[...] * result
    for j in range(8):
        out_ref[pl.ds(j, 32, stride=8), :] = out[j * 32 : (j + 1) * 32]


def call(kernel, outputs, scratch, scalars, *blocks):
    specs = [pl.BlockSpec(memory_space=pltpu.SMEM)] * len(scalars)
    specs += [pl.BlockSpec(memory_space=pltpu.VMEM)] * len(blocks)
    return pl.pallas_call(
        kernel,
        out_shape=[jax.ShapeDtypeStruct(shape, jnp.float32) for shape in outputs],
        in_specs=specs,
        out_specs=[pl.BlockSpec(memory_space=pltpu.VMEM)] * len(outputs),
        scratch_shapes=scratch,
        compiler_params=pltpu.CompilerParams(vmem_limit_bytes=VMEM_LIMIT),
    )(*scalars, *blocks)


def exchange(value, axis, distance):
    count = lax.axis_size(axis)
    return lax.ppermute(value, axis, [(n, n ^ distance) for n in range(count)])


def far_first(rows, columns):
    return [(row ^ FAR_ROW, column ^ FAR_COLUMN) for row in range(rows) for column in range(columns)]


def exchange_groups(rows, columns):
    places = far_first(rows, columns)
    return [[(row * columns + column) * 2 + core for row, column in places] for core in range(2)]


def gather_groups(rows, columns):
    place = lambda row, column, core: (row * columns + column) * 2 + core
    first = [
        [place(row, column ^ FAR_COLUMN, 0) for column in range(columns)] for row in range(rows)
    ]
    second = [
        [place(row ^ FAR_ROW, column + n, 1) for n in range(2) for row in range(rows)]
        for column in range(0, columns, 2)
    ]
    return first + second


def per_device(
    pair,
    alignment_left,
    alignment_right,
    outer_mean_weight,
    outer_mean_bias,
    input_norm_gain,
    input_norm_bias,
    input_weight_matrix,
    input_bias_vector,
    output_norm_gain,
    output_norm_bias,
    output_weight_matrix,
    output_bias_vector,
):
    rows, columns = lax.axis_size("row"), lax.axis_size("col")

    def spread(value, groups):
        return lax.all_to_all(
            value, ("row", "col", "seq"), 0, 0, tiled=True, axis_index_groups=groups
        )

    core = lax.axis_index("seq")
    place = jnp.stack([core, lax.axis_index("col") % 2])
    core_array = core.reshape(1)
    left = alignment_left.transpose(1, 2, 0).reshape(64, 64)
    right = alignment_right.transpose(1, 2, 0).reshape(64, 64)
    kept = jnp.where(core == 0, left, right)
    vectors = [
        outer_mean_bias,
        input_norm_gain,
        input_norm_bias,
        output_norm_gain,
        output_norm_bias,
        output_bias_vector,
        input_bias_vector,
    ]
    vectors = jnp.concatenate([vector.reshape(-1, LANES) for vector in vectors], axis=0)
    (blocks,) = call(
        pack_kernel,
        [(1024, LANES)],
        [],
        [core_array],
        kept,
        exchange(left, "seq", 1),
        exchange(right, "seq", 1),
    )
    own = spread(blocks, gather_groups(rows, columns))
    send, updated, gate = call(
        tile_kernel,
        [(512, LANES), (256, LANES), (256, LANES)],
        [
            pltpu.VMEM((256, LANES), jnp.float32),
            pltpu.VMEM((256, 1024), jnp.bfloat16),
            pltpu.VMEM((256, 1024), jnp.bfloat16),
        ],
        [place],
        own,
        exchange(own, "seq", 1),
        pair.reshape(256, LANES),
        outer_mean_weight,
        input_weight_matrix,
        vectors,
    )
    own = spread(send, exchange_groups(rows, columns))
    (back,) = call(
        triangle_kernel,
        [(256, LANES)],
        [
            pltpu.VMEM((2, 256, LANES), jnp.float32),
            pltpu.VMEM((2, 128, LANES), jnp.float32),
        ],
        [core_array],
        own,
        exchange(own, "seq", 1),
    )
    mixed = spread(back, exchange_groups(rows, columns))
    (out,) = call(
        output_kernel,
        [(256, LANES)],
        [],
        [],
        mixed,
        updated,
        gate,
        output_weight_matrix,
        vectors,
    )
    return out.reshape(pair.shape)


def solution(mesh):
    return jax.shard_map(
        per_device,
        mesh=mesh,
        in_specs=(
            P("row", ("col", "seq"), None),
            P("seq", "row", "col"),
            P("seq", "col", "row"),
            P(),
            P(),
            P(),
            P(),
            P(),
            P(),
            P(),
            P(),
            P(),
            P(),
        ),
        out_specs=P("row", ("col", "seq"), None),
        check_vma=False,
    )
```

```python
import functools

import jax
import jax.numpy as jnp
from jax import lax
from jax.experimental import pallas as pl
from jax.experimental.pallas import tpu as pltpu
from jax.sharding import PartitionSpec as P

SEQUENCE_COUNT = 128
EPSILON = 1e-05
LANES = 128
VMEM_LIMIT = 32 * 1024 * 1024
FAR_ROW, FAR_COLUMN = 4, 10


def split(value):
    high = value.astype(jnp.bfloat16)
    return high, (value - high.astype(jnp.float32)).astype(jnp.bfloat16)


def product(left, right, transposed):
    dims = (((1,), (1 if transposed else 0,)), ((), ()))
    dot = functools.partial(
        lax.dot_general, dimension_numbers=dims, preferred_element_type=jnp.float32
    )
    if left[0].shape[1] == LANES:
        return dot(
            jnp.concatenate([left[0], left[1], left[0]], axis=1),
            jnp.concatenate([right[0], right[0], right[1]], axis=1 if transposed else 0),
        )
    if right[0].shape[1] == LANES and not transposed:
        both = dot(left[0], jnp.concatenate([right[0], right[1]], axis=1))
        return both[:, :LANES] + (both[:, LANES:] + dot(left[1], right[0]))
    return dot(left[0], right[0]) + (dot(left[0], right[1]) + dot(left[1], right[0]))


def swap_groups(blocks):
    lane = lax.broadcasted_iota(jnp.int32, blocks[0].shape, 1)
    wide, narrow = (lane & 64) == 0, (lane & 32) == 0

    def exchange(first, second, shift, mask):
        return (
            jnp.where(mask, first, pltpu.roll(second, shift, 1)),
            jnp.where(mask, pltpu.roll(first, LANES - shift, 1), second),
        )

    a, c = exchange(blocks[0], blocks[2], 64, wide)
    b, d = exchange(blocks[1], blocks[3], 64, wide)
    a, b = exchange(a, b, 32, narrow)
    c, d = exchange(c, d, 32, narrow)
    return a, b, c, d


def pack_kernel(core_ref, kept_ref, left_ref, right_ref, out_ref):
    first_core = core_ref[0] == 0

    def ordered(left_ref, right_ref):
        left = [left_ref[pl.ds(p, 32, stride=2), :] for p in range(2)]
        right = [right_ref[pl.ds(q, 16, stride=4), :] for q in range(4)]
        return jnp.where(first_core, jnp.concatenate(right, axis=0), jnp.concatenate(left, axis=0))

    kept, got = ordered(kept_ref, kept_ref), ordered(left_ref, right_ref)
    lower, upper = jnp.where(first_core, kept, got), jnp.where(first_core, got, kept)
    block = jnp.concatenate([lower, upper], axis=1)
    for n in range(16):
        out_ref[pl.ds(n * 64, 64), :] = block


def tile_kernel(
    place_ref,
    own_ref,
    other_ref,
    pair_ref,
    mean_weight_ref,
    weight_ref,
    vectors_ref,
    send_ref,
    updated_ref,
    gate_ref,
    right_scratch,
    high_scratch,
    low_scratch,
):
    core, odd = place_ref[0], place_ref[1]
    first_core = core == 0
    for row in range(8):
        for q in range(4):
            start = odd * 512 + row * 64 + q * 16 + core * 8
            rows = pl.ds(pl.multiple_of(start, 8), 8)
            right_scratch[pl.ds((row ^ FAR_ROW) * 32 + q * 8, 8), :] = jnp.where(
                first_core, own_ref[rows, :], other_ref[rows, :]
            )
    right = split(
        jnp.concatenate([right_scratch[pl.ds(j, 32, stride=8), :] for j in range(8)], axis=0)
    )
    left = jnp.where(first_core, other_ref[...], own_ref[...])
    outer = [product(split(left[n * 512 : (n + 1) * 512]), right, True) for n in range(2)]
    for group in range(8):
        for wide in range(2):
            blocks = [
                outer[group // 4][
                    (group % 4 * 4 + p) * 32 : (group % 4 * 4 + p + 1) * 32,
                    wide * LANES : (wide + 1) * LANES,
                ]
                for p in range(4)
            ]
            for j, block in enumerate(swap_groups(blocks)):
                rows = pl.ds((wide * 4 + j) * 32, 32)
                columns = pl.ds((group ^ (FAR_COLUMN // 2)) * LANES, LANES)
                high, low = split(block)
                high_scratch[rows, columns] = high
                low_scratch[rows, columns] = low
    summed = product(
        (high_scratch[...], low_scratch[...]), split(mean_weight_ref[...]), False
    )
    pair = jnp.concatenate([pair_ref[pl.ds(j, 32, stride=8), :] for j in range(8)], axis=0)
    updated = pair + (summed + vectors_ref[0:1]) * (1.0 / SEQUENCE_COUNT)
    updated_ref[...] = updated
    center = updated - jnp.mean(updated, axis=1, keepdims=True)
    spread = jnp.mean(center * center, axis=1, keepdims=True)
    normed = center * lax.rsqrt(spread + EPSILON) * vectors_ref[1:2] + vectors_ref[2:3]
    proj = product(split(normed), split(weight_ref[...]), False)
    blocks = [
        proj[:, n * LANES : (n + 1) * LANES] + vectors_ref[6 + n : 7 + n] for n in range(5)
    ]
    left_act = jnp.transpose(jax.nn.sigmoid(blocks[1]) * blocks[0])
    right_act = jnp.transpose(jax.nn.sigmoid(blocks[3]) * blocks[2])
    send_ref[pl.ds(0, 128, stride=4), :] = left_act[:, :LANES]
    send_ref[pl.ds(1, 128, stride=4), :] = left_act[:, LANES:]
    send_ref[pl.ds(2, 128, stride=4), :] = right_act[:, :LANES]
    send_ref[pl.ds(3, 128, stride=4), :] = right_act[:, LANES:]
    gate_ref[...] = jax.nn.sigmoid(blocks[4])


def triangle_kernel(core_ref, own_ref, other_ref, send_ref, left_scratch, right_scratch):
    first_core = core_ref[0] == 0

    def regroup(source, part, wide):
        return swap_groups([source(wide * 4 + r, part) for r in range(4)])

    def rows_of(ref):
        return lambda r, part: ref[pl.ds(r * 64 + part, 16, stride=4), :]

    own, other = rows_of(own_ref), rows_of(other_ref)

    def lower(r, part):
        return jnp.where(first_core, own(r, part), other(r, part))

    def upper(r, part):
        return jnp.where(first_core, other(r, part), own(r, part))

    for wide in range(2):
        for part in range(2):
            for core, source in enumerate((lower, upper)):
                for g, block in enumerate(regroup(source, part, wide)):
                    place = core * 8 + part * 4 + g
                    left_scratch[wide, pl.ds(place, 16, stride=16), :] = block
            for g, block in enumerate(regroup(own, part + 2, wide)):
                right_scratch[wide, pl.ds((part * 4 + g) * 16, 16), :] = block
    left = split(jnp.concatenate([left_scratch[0], left_scratch[1]], axis=1))
    right = split(jnp.concatenate([right_scratch[0], right_scratch[1]], axis=1))
    mixed = product(right, left, True)
    for wide in range(2):
        for part in range(2):
            blocks = [
                mixed[
                    (part * 4 + g) * 16 : (part * 4 + g + 1) * 16,
                    wide * LANES : (wide + 1) * LANES,
                ]
                for g in range(4)
            ]
            for r, block in enumerate(swap_groups(blocks)):
                place = (wide * 4 + r) ^ (FAR_COLUMN // 2) ^ FAR_ROW
                send_ref[pl.ds(place * 32 + part, 16, stride=2), :] = block


def output_kernel(mixed_ref, updated_ref, gate_ref, weight_ref, vectors_ref, out_ref):
    mixed = jnp.concatenate(
        [mixed_ref[pl.ds(0, 128, stride=2), :], mixed_ref[pl.ds(1, 128, stride=2), :]], axis=1
    )
    center = mixed - jnp.mean(mixed, axis=0, keepdims=True)
    spread = jnp.mean(center * center, axis=0, keepdims=True)
    normed = jnp.transpose(center * lax.rsqrt(spread + EPSILON))
    normed = normed * vectors_ref[3:4] + vectors_ref[4:5]
    result = product(split(normed), split(weight_ref[...]), False) + vectors_ref[5:6]
    out = updated_ref[...] + gate_ref[...] * result
    for j in range(8):
        out_ref[pl.ds(j, 32, stride=8), :] = out[j * 32 : (j + 1) * 32]


def call(kernel, outputs, scratch, scalars, *blocks):
    specs = [pl.BlockSpec(memory_space=pltpu.SMEM)] * len(scalars)
    specs += [pl.BlockSpec(memory_space=pltpu.VMEM)] * len(blocks)
    return pl.pallas_call(
        kernel,
        out_shape=[jax.ShapeDtypeStruct(shape, jnp.float32) for shape in outputs],
        in_specs=specs,
        out_specs=[pl.BlockSpec(memory_space=pltpu.VMEM)] * len(outputs),
        scratch_shapes=scratch,
        compiler_params=pltpu.CompilerParams(vmem_limit_bytes=VMEM_LIMIT),
    )(*scalars, *blocks)


def exchange(value, axis, distance):
    count = lax.axis_size(axis)
    return lax.ppermute(value, axis, [(n, n ^ distance) for n in range(count)])


def far_first(rows, columns):
    return [(row ^ FAR_ROW, column ^ FAR_COLUMN) for row in range(rows) for column in range(columns)]


def exchange_groups(rows, columns):
    places = far_first(rows, columns)
    return [[(row * columns + column) * 2 + core for row, column in places] for core in range(2)]


def gather_groups(rows, columns):
    place = lambda row, column, core: (row * columns + column) * 2 + core
    first = [
        [place(row, column ^ FAR_COLUMN, 1) for column in range(columns)] for row in range(rows)
    ]
    second = [
        [place(row ^ FAR_ROW, column + n, 0) for n in range(2) for row in range(rows)]
        for column in range(0, columns, 2)
    ]
    return first + second


def per_device(
    pair,
    alignment_left,
    alignment_right,
    outer_mean_weight,
    outer_mean_bias,
    input_norm_gain,
    input_norm_bias,
    input_weight_matrix,
    input_bias_vector,
    output_norm_gain,
    output_norm_bias,
    output_weight_matrix,
    output_bias_vector,
):
    rows, columns = lax.axis_size("row"), lax.axis_size("col")

    def spread(value, groups):
        return lax.all_to_all(
            value, ("row", "col", "seq"), 0, 0, tiled=True, axis_index_groups=groups
        )

    core = lax.axis_index("seq")
    place = jnp.stack([core, lax.axis_index("col") % 2])
    core_array = core.reshape(1)
    left = alignment_left.transpose(1, 2, 0).reshape(64, 64)
    right = alignment_right.transpose(1, 2, 0).reshape(64, 64)
    kept = jnp.where(core == 0, right, left)
    vectors = [
        outer_mean_bias,
        input_norm_gain,
        input_norm_bias,
        output_norm_gain,
        output_norm_bias,
        output_bias_vector,
        input_bias_vector,
    ]
    vectors = jnp.concatenate([vector.reshape(-1, LANES) for vector in vectors], axis=0)
    (blocks,) = call(
        pack_kernel,
        [(1024, LANES)],
        [],
        [core_array],
        kept,
        exchange(left, "seq", 1),
        exchange(right, "seq", 1),
    )
    own = spread(blocks, gather_groups(rows, columns))
    send, updated, gate = call(
        tile_kernel,
        [(512, LANES), (256, LANES), (256, LANES)],
        [
            pltpu.VMEM((256, LANES), jnp.float32),
            pltpu.VMEM((256, 1024), jnp.bfloat16),
            pltpu.VMEM((256, 1024), jnp.bfloat16),
        ],
        [place],
        own,
        exchange(own, "seq", 1),
        pair.reshape(256, LANES),
        outer_mean_weight,
        input_weight_matrix,
        vectors,
    )
    own = spread(send, exchange_groups(rows, columns))
    (back,) = call(
        triangle_kernel,
        [(256, LANES)],
        [
            pltpu.VMEM((2, 256, LANES), jnp.float32),
            pltpu.VMEM((2, 128, LANES), jnp.float32),
        ],
        [core_array],
        own,
        exchange(own, "seq", 1),
    )
    mixed = spread(back, exchange_groups(rows, columns))
    (out,) = call(
        output_kernel,
        [(256, LANES)],
        [],
        [],
        mixed,
        updated,
        gate,
        output_weight_matrix,
        vectors,
    )
    return out.reshape(pair.shape)


def solution(mesh):
    return jax.shard_map(
        per_device,
        mesh=mesh,
        in_specs=(
            P("row", ("col", "seq"), None),
            P("seq", "row", "col"),
            P("seq", "col", "row"),
            P(),
            P(),
            P(),
            P(),
            P(),
            P(),
            P(),
            P(),
            P(),
            P(),
        ),
        out_specs=P("row", ("col", "seq"), None),
        check_vma=False,
    )
```

```python
import functools

import jax
import jax.numpy as jnp
from jax import lax
from jax.experimental import pallas as pl
from jax.experimental.pallas import tpu as pltpu
from jax.sharding import PartitionSpec as P

SEQUENCE_COUNT = 128
EPSILON = 1e-05
LANES = 128
VMEM_LIMIT = 32 * 1024 * 1024
GATHER_ROW, OUT_ROW, BACK_ROW, FAR_COLUMN = 5, 7, 6, 10


def split(value):
    high = value.astype(jnp.bfloat16)
    return high, (value - high.astype(jnp.float32)).astype(jnp.bfloat16)


def product(left, right, transposed):
    dims = (((1,), (1 if transposed else 0,)), ((), ()))
    dot = functools.partial(
        lax.dot_general, dimension_numbers=dims, preferred_element_type=jnp.float32
    )
    if left[0].shape[1] == LANES:
        return dot(
            jnp.concatenate([left[0], left[1], left[0]], axis=1),
            jnp.concatenate([right[0], right[0], right[1]], axis=1 if transposed else 0),
        )
    if right[0].shape[1] == LANES and not transposed:
        both = dot(left[0], jnp.concatenate([right[0], right[1]], axis=1))
        return both[:, :LANES] + (both[:, LANES:] + dot(left[1], right[0]))
    return dot(left[0], right[0]) + (dot(left[0], right[1]) + dot(left[1], right[0]))


def swap_groups(blocks):
    lane = lax.broadcasted_iota(jnp.int32, blocks[0].shape, 1)
    wide, narrow = (lane & 64) == 0, (lane & 32) == 0

    def exchange(first, second, shift, mask):
        return (
            jnp.where(mask, first, pltpu.roll(second, shift, 1)),
            jnp.where(mask, pltpu.roll(first, LANES - shift, 1), second),
        )

    a, c = exchange(blocks[0], blocks[2], 64, wide)
    b, d = exchange(blocks[1], blocks[3], 64, wide)
    a, b = exchange(a, b, 32, narrow)
    c, d = exchange(c, d, 32, narrow)
    return a, b, c, d


def pack_kernel(core_ref, kept_ref, left_ref, right_ref, out_ref):
    first_core = core_ref[0] == 0

    def ordered(left_ref, right_ref):
        left = [left_ref[pl.ds(p, 32, stride=2), :] for p in range(2)]
        right = [right_ref[pl.ds(q, 16, stride=4), :] for q in range(4)]
        return jnp.where(first_core, jnp.concatenate(right, axis=0), jnp.concatenate(left, axis=0))

    kept, got = ordered(kept_ref, kept_ref), ordered(left_ref, right_ref)
    lower, upper = jnp.where(first_core, kept, got), jnp.where(first_core, got, kept)
    block = jnp.concatenate([lower, upper], axis=1)
    for n in range(16):
        out_ref[pl.ds(n * 64, 64), :] = block


def tile_kernel(
    place_ref,
    own_ref,
    other_ref,
    pair_ref,
    mean_weight_ref,
    weight_ref,
    vectors_ref,
    send_ref,
    updated_ref,
    gate_ref,
    right_scratch,
    high_scratch,
    low_scratch,
):
    core, odd = place_ref[0], place_ref[1]
    first_core = core == 0
    for row in range(8):
        for q in range(4):
            start = odd * 512 + row * 64 + q * 16 + core * 8
            rows = pl.ds(pl.multiple_of(start, 8), 8)
            right_scratch[pl.ds((row ^ GATHER_ROW) * 32 + q * 8, 8), :] = jnp.where(
                first_core, own_ref[rows, :], other_ref[rows, :]
            )
    right = split(
        jnp.concatenate([right_scratch[pl.ds(j, 32, stride=8), :] for j in range(8)], axis=0)
    )
    left = jnp.where(first_core, other_ref[...], own_ref[...])
    outer = [product(split(left[n * 512 : (n + 1) * 512]), right, True) for n in range(2)]
    for group in range(8):
        for wide in range(2):
            blocks = [
                outer[group // 4][
                    (group % 4 * 4 + p) * 32 : (group % 4 * 4 + p + 1) * 32,
                    wide * LANES : (wide + 1) * LANES,
                ]
                for p in range(4)
            ]
            for j, block in enumerate(swap_groups(blocks)):
                rows = pl.ds((wide * 4 + j) * 32, 32)
                columns = pl.ds((group ^ (FAR_COLUMN // 2)) * LANES, LANES)
                high, low = split(block)
                high_scratch[rows, columns] = high
                low_scratch[rows, columns] = low
    summed = product(
        (high_scratch[...], low_scratch[...]), split(mean_weight_ref[...]), False
    )
    pair = jnp.concatenate([pair_ref[pl.ds(j, 32, stride=8), :] for j in range(8)], axis=0)
    updated = pair + (summed + vectors_ref[0:1]) * (1.0 / SEQUENCE_COUNT)
    updated_ref[...] = updated
    center = updated - jnp.mean(updated, axis=1, keepdims=True)
    spread = jnp.mean(center * center, axis=1, keepdims=True)
    normed = center * lax.rsqrt(spread + EPSILON) * vectors_ref[1:2] + vectors_ref[2:3]
    proj = product(split(normed), split(weight_ref[...]), False)
    blocks = [
        proj[:, n * LANES : (n + 1) * LANES] + vectors_ref[6 + n : 7 + n] for n in range(5)
    ]
    left_act = jnp.transpose(jax.nn.sigmoid(blocks[1]) * blocks[0])
    right_act = jnp.transpose(jax.nn.sigmoid(blocks[3]) * blocks[2])
    for n in range(8):
        channels = slice(n * 16, (n + 1) * 16)
        begin = (n ^ OUT_ROW ^ BACK_ROW) * 64
        send_ref[pl.ds(begin, 16, stride=4), :] = left_act[channels, :LANES]
        send_ref[pl.ds(begin + 1, 16, stride=4), :] = left_act[channels, LANES:]
        send_ref[pl.ds(begin + 2, 16, stride=4), :] = right_act[channels, :LANES]
        send_ref[pl.ds(begin + 3, 16, stride=4), :] = right_act[channels, LANES:]
    gate_ref[...] = jax.nn.sigmoid(blocks[4])


def triangle_kernel(core_ref, own_ref, other_ref, send_ref, left_scratch, right_scratch):
    first_core = core_ref[0] == 0

    def regroup(source, part, wide):
        return swap_groups([source(wide * 4 + r, part) for r in range(4)])

    def rows_of(ref):
        return lambda r, part: ref[pl.ds(r * 64 + part, 16, stride=4), :]

    own, other = rows_of(own_ref), rows_of(other_ref)

    def lower(r, part):
        return jnp.where(first_core, own(r, part), other(r, part))

    def upper(r, part):
        return jnp.where(first_core, other(r, part), own(r, part))

    for wide in range(2):
        for part in range(2):
            for core, source in enumerate((lower, upper)):
                for g, block in enumerate(regroup(source, part, wide)):
                    place = core * 8 + part * 4 + g
                    left_scratch[wide, pl.ds(place, 16, stride=16), :] = block
            for g, block in enumerate(regroup(own, part + 2, wide)):
                right_scratch[wide, pl.ds((part * 4 + g) * 16, 16), :] = block
    left = split(jnp.concatenate([left_scratch[0], left_scratch[1]], axis=1))
    right = split(jnp.concatenate([right_scratch[0], right_scratch[1]], axis=1))
    mixed = product(right, left, True)
    for wide in range(2):
        for part in range(2):
            blocks = [
                mixed[
                    (part * 4 + g) * 16 : (part * 4 + g + 1) * 16,
                    wide * LANES : (wide + 1) * LANES,
                ]
                for g in range(4)
            ]
            for r, block in enumerate(swap_groups(blocks)):
                place = (wide * 4 + r) ^ (FAR_COLUMN // 2) ^ BACK_ROW
                send_ref[pl.ds(place * 32 + part, 16, stride=2), :] = block


def output_kernel(mixed_ref, updated_ref, gate_ref, weight_ref, vectors_ref, out_ref):
    mixed = jnp.concatenate(
        [mixed_ref[pl.ds(0, 128, stride=2), :], mixed_ref[pl.ds(1, 128, stride=2), :]], axis=1
    )
    center = mixed - jnp.mean(mixed, axis=0, keepdims=True)
    spread = jnp.mean(center * center, axis=0, keepdims=True)
    normed = jnp.transpose(center * lax.rsqrt(spread + EPSILON))
    normed = normed * vectors_ref[3:4] + vectors_ref[4:5]
    result = product(split(normed), split(weight_ref[...]), False) + vectors_ref[5:6]
    out = updated_ref[...] + gate_ref[...] * result
    for j in range(8):
        out_ref[pl.ds(j, 32, stride=8), :] = out[j * 32 : (j + 1) * 32]


def call(kernel, outputs, scratch, scalars, *blocks):
    specs = [pl.BlockSpec(memory_space=pltpu.SMEM)] * len(scalars)
    specs += [pl.BlockSpec(memory_space=pltpu.VMEM)] * len(blocks)
    return pl.pallas_call(
        kernel,
        out_shape=[jax.ShapeDtypeStruct(shape, jnp.float32) for shape in outputs],
        in_specs=specs,
        out_specs=[pl.BlockSpec(memory_space=pltpu.VMEM)] * len(outputs),
        scratch_shapes=scratch,
        compiler_params=pltpu.CompilerParams(vmem_limit_bytes=VMEM_LIMIT),
    )(*scalars, *blocks)


def exchange(value, axis, distance):
    count = lax.axis_size(axis)
    return lax.ppermute(value, axis, [(n, n ^ distance) for n in range(count)])


def exchange_groups(rows, columns, mask):
    return [
        [
            ((row ^ mask) * columns + (column ^ FAR_COLUMN)) * 2 + core
            for row in range(rows)
            for column in range(columns)
        ]
        for core in range(2)
    ]


def gather_groups(rows, columns):
    place = lambda row, column, core: (row * columns + column) * 2 + core
    first = [
        [place(row, column ^ FAR_COLUMN, 1) for column in range(columns)] for row in range(rows)
    ]
    second = [
        [place(row ^ GATHER_ROW, column + n, 0) for n in range(2) for row in range(rows)]
        for column in range(0, columns, 2)
    ]
    return first + second


def per_device(
    pair,
    alignment_left,
    alignment_right,
    outer_mean_weight,
    outer_mean_bias,
    input_norm_gain,
    input_norm_bias,
    input_weight_matrix,
    input_bias_vector,
    output_norm_gain,
    output_norm_bias,
    output_weight_matrix,
    output_bias_vector,
):
    rows, columns = lax.axis_size("row"), lax.axis_size("col")

    def spread(value, groups):
        return lax.all_to_all(
            value, ("row", "col", "seq"), 0, 0, tiled=True, axis_index_groups=groups
        )

    core = lax.axis_index("seq")
    place = jnp.stack([core, lax.axis_index("col") % 2])
    core_array = core.reshape(1)
    left = alignment_left.transpose(1, 2, 0).reshape(64, 64)
    right = alignment_right.transpose(1, 2, 0).reshape(64, 64)
    kept = jnp.where(core == 0, right, left)
    vectors = [
        outer_mean_bias,
        input_norm_gain,
        input_norm_bias,
        output_norm_gain,
        output_norm_bias,
        output_bias_vector,
        input_bias_vector,
    ]
    vectors = jnp.concatenate([vector.reshape(-1, LANES) for vector in vectors], axis=0)
    (blocks,) = call(
        pack_kernel,
        [(1024, LANES)],
        [],
        [core_array],
        kept,
        exchange(left, "seq", 1),
        exchange(right, "seq", 1),
    )
    own = spread(blocks, gather_groups(rows, columns))
    send, updated, gate = call(
        tile_kernel,
        [(512, LANES), (256, LANES), (256, LANES)],
        [
            pltpu.VMEM((256, LANES), jnp.float32),
            pltpu.VMEM((256, 1024), jnp.bfloat16),
            pltpu.VMEM((256, 1024), jnp.bfloat16),
        ],
        [place],
        own,
        exchange(own, "seq", 1),
        pair.reshape(256, LANES),
        outer_mean_weight,
        input_weight_matrix,
        vectors,
    )
    own = spread(send, exchange_groups(rows, columns, OUT_ROW))
    (back,) = call(
        triangle_kernel,
        [(256, LANES)],
        [
            pltpu.VMEM((2, 256, LANES), jnp.float32),
            pltpu.VMEM((2, 128, LANES), jnp.float32),
        ],
        [core_array],
        own,
        exchange(own, "seq", 1),
    )
    mixed = spread(back, exchange_groups(rows, columns, BACK_ROW))
    (out,) = call(
        output_kernel,
        [(256, LANES)],
        [],
        [],
        mixed,
        updated,
        gate,
        output_weight_matrix,
        vectors,
    )
    return out.reshape(pair.shape)


def solution(mesh):
    return jax.shard_map(
        per_device,
        mesh=mesh,
        in_specs=(
            P("row", ("col", "seq"), None),
            P("seq", "row", "col"),
            P("seq", "col", "row"),
            P(),
            P(),
            P(),
            P(),
            P(),
            P(),
            P(),
            P(),
            P(),
            P(),
        ),
        out_specs=P("row", ("col", "seq"), None),
        check_vma=False,
    )
```

```python
import functools

import jax
import jax.numpy as jnp
from jax import lax
from jax.experimental import pallas as pl
from jax.experimental.pallas import tpu as pltpu
from jax.sharding import PartitionSpec as P

SEQUENCE_COUNT = 128
EPSILON = 1e-05
LANES = 128
VMEM_LIMIT = 32 * 1024 * 1024
GATHER_ROW, OUT_ROW, BACK_ROW, FAR_COLUMN = 5, 7, 6, 10


def split(value):
    high = value.astype(jnp.bfloat16)
    return high, (value - high.astype(jnp.float32)).astype(jnp.bfloat16)


def product(left, right, transposed):
    dims = (((1,), (1 if transposed else 0,)), ((), ()))
    dot = functools.partial(
        lax.dot_general, dimension_numbers=dims, preferred_element_type=jnp.float32
    )
    if left[0].shape[1] == LANES:
        return dot(
            jnp.concatenate([left[0], left[1], left[0]], axis=1),
            jnp.concatenate([right[0], right[0], right[1]], axis=1 if transposed else 0),
        )
    if right[0].shape[1] == LANES and not transposed:
        both = dot(left[0], jnp.concatenate([right[0], right[1]], axis=1))
        return both[:, :LANES] + (both[:, LANES:] + dot(left[1], right[0]))
    return dot(left[0], right[0]) + (dot(left[0], right[1]) + dot(left[1], right[0]))


def swap_groups(blocks):
    lane = lax.broadcasted_iota(jnp.int32, blocks[0].shape, 1)
    wide, narrow = (lane & 64) == 0, (lane & 32) == 0

    def exchange(first, second, shift, mask):
        return (
            jnp.where(mask, first, pltpu.roll(second, shift, 1)),
            jnp.where(mask, pltpu.roll(first, LANES - shift, 1), second),
        )

    a, c = exchange(blocks[0], blocks[2], 64, wide)
    b, d = exchange(blocks[1], blocks[3], 64, wide)
    a, b = exchange(a, b, 32, narrow)
    c, d = exchange(c, d, 32, narrow)
    return a, b, c, d


def pack_kernel(kept_ref, left_ref, right_ref, out_ref):
    first_core = lax.axis_index("seq") == 0

    def ordered(left_ref, right_ref):
        left = [left_ref[pl.ds(p, 32, stride=2), :] for p in range(2)]
        right = [right_ref[pl.ds(q, 16, stride=4), :] for q in range(4)]
        return jnp.where(first_core, jnp.concatenate(right, axis=0), jnp.concatenate(left, axis=0))

    kept, got = ordered(kept_ref, kept_ref), ordered(left_ref, right_ref)
    lower, upper = jnp.where(first_core, kept, got), jnp.where(first_core, got, kept)
    block = jnp.concatenate([lower, upper], axis=1)
    for n in range(16):
        out_ref[pl.ds(n * 64, 64), :] = block


def tile_kernel(
    own_ref,
    other_ref,
    pair_ref,
    mean_weight_ref,
    weight_ref,
    vectors_ref,
    send_ref,
    updated_ref,
    gate_ref,
    right_scratch,
    high_scratch,
    low_scratch,
):
    core, odd = lax.axis_index("seq"), lax.rem(lax.axis_index("col"), 2)
    first_core = core == 0
    for row in range(8):
        for q in range(4):
            start = odd * 512 + row * 64 + q * 16 + core * 8
            rows = pl.ds(pl.multiple_of(start, 8), 8)
            right_scratch[pl.ds((row ^ GATHER_ROW) * 32 + q * 8, 8), :] = jnp.where(
                first_core, own_ref[rows, :], other_ref[rows, :]
            )
    right = split(
        jnp.concatenate([right_scratch[pl.ds(j, 32, stride=8), :] for j in range(8)], axis=0)
    )
    left = jnp.where(first_core, other_ref[...], own_ref[...])
    outer = [product(split(left[n * 512 : (n + 1) * 512]), right, True) for n in range(2)]
    for group in range(8):
        for wide in range(2):
            blocks = [
                outer[group // 4][
                    (group % 4 * 4 + p) * 32 : (group % 4 * 4 + p + 1) * 32,
                    wide * LANES : (wide + 1) * LANES,
                ]
                for p in range(4)
            ]
            for j, block in enumerate(swap_groups(blocks)):
                rows = pl.ds((wide * 4 + j) * 32, 32)
                columns = pl.ds((group ^ (FAR_COLUMN // 2)) * LANES, LANES)
                high, low = split(block)
                high_scratch[rows, columns] = high
                low_scratch[rows, columns] = low
    summed = product(
        (high_scratch[...], low_scratch[...]), split(mean_weight_ref[...]), False
    )
    pair = jnp.concatenate([pair_ref[pl.ds(j, 32, stride=8), :] for j in range(8)], axis=0)
    updated = pair + (summed + vectors_ref[0:1]) * (1.0 / SEQUENCE_COUNT)
    updated_ref[...] = updated
    center = updated - jnp.mean(updated, axis=1, keepdims=True)
    spread = jnp.mean(center * center, axis=1, keepdims=True)
    normed = center * lax.rsqrt(spread + EPSILON) * vectors_ref[1:2] + vectors_ref[2:3]
    proj = product(split(normed), split(weight_ref[...]), False)
    blocks = [
        proj[:, n * LANES : (n + 1) * LANES] + vectors_ref[6 + n : 7 + n] for n in range(5)
    ]
    left_act = jnp.transpose(jax.nn.sigmoid(blocks[1]) * blocks[0])
    right_act = jnp.transpose(jax.nn.sigmoid(blocks[3]) * blocks[2])
    for n in range(8):
        channels = slice(n * 16, (n + 1) * 16)
        begin = (n ^ OUT_ROW ^ BACK_ROW) * 64
        send_ref[pl.ds(begin, 16, stride=4), :] = left_act[channels, :LANES]
        send_ref[pl.ds(begin + 1, 16, stride=4), :] = left_act[channels, LANES:]
        send_ref[pl.ds(begin + 2, 16, stride=4), :] = right_act[channels, :LANES]
        send_ref[pl.ds(begin + 3, 16, stride=4), :] = right_act[channels, LANES:]
    gate_ref[...] = jax.nn.sigmoid(blocks[4])


def triangle_kernel(own_ref, other_ref, send_ref, left_scratch, right_scratch):
    first_core = lax.axis_index("seq") == 0

    def regroup(source, part, wide):
        return swap_groups([source(wide * 4 + r, part) for r in range(4)])

    def rows_of(ref):
        return lambda r, part: ref[pl.ds(r * 64 + part, 16, stride=4), :]

    own, other = rows_of(own_ref), rows_of(other_ref)

    def lower(r, part):
        return jnp.where(first_core, own(r, part), other(r, part))

    def upper(r, part):
        return jnp.where(first_core, other(r, part), own(r, part))

    for wide in range(2):
        for part in range(2):
            for core, source in enumerate((lower, upper)):
                for g, block in enumerate(regroup(source, part, wide)):
                    place = core * 8 + part * 4 + g
                    left_scratch[wide, pl.ds(place, 16, stride=16), :] = block
            for g, block in enumerate(regroup(own, part + 2, wide)):
                right_scratch[wide, pl.ds((part * 4 + g) * 16, 16), :] = block
    left = split(jnp.concatenate([left_scratch[0], left_scratch[1]], axis=1))
    right = split(jnp.concatenate([right_scratch[0], right_scratch[1]], axis=1))
    mixed = product(right, left, True)
    for wide in range(2):
        for part in range(2):
            blocks = [
                mixed[
                    (part * 4 + g) * 16 : (part * 4 + g + 1) * 16,
                    wide * LANES : (wide + 1) * LANES,
                ]
                for g in range(4)
            ]
            for r, block in enumerate(swap_groups(blocks)):
                place = (wide * 4 + r) ^ (FAR_COLUMN // 2) ^ BACK_ROW
                send_ref[pl.ds(place * 32 + part, 16, stride=2), :] = block


def output_kernel(mixed_ref, updated_ref, gate_ref, weight_ref, vectors_ref, out_ref):
    mixed = jnp.concatenate(
        [mixed_ref[pl.ds(0, 128, stride=2), :], mixed_ref[pl.ds(1, 128, stride=2), :]], axis=1
    )
    center = mixed - jnp.mean(mixed, axis=0, keepdims=True)
    spread = jnp.mean(center * center, axis=0, keepdims=True)
    normed = jnp.transpose(center * lax.rsqrt(spread + EPSILON))
    normed = normed * vectors_ref[3:4] + vectors_ref[4:5]
    result = product(split(normed), split(weight_ref[...]), False) + vectors_ref[5:6]
    out = updated_ref[...] + gate_ref[...] * result
    for j in range(8):
        out_ref[pl.ds(j, 32, stride=8), :] = out[j * 32 : (j + 1) * 32]


def call(kernel, outputs, scratch, *blocks):
    return pl.pallas_call(
        kernel,
        out_shape=[jax.ShapeDtypeStruct(shape, jnp.float32) for shape in outputs],
        in_specs=[pl.BlockSpec(memory_space=pltpu.VMEM)] * len(blocks),
        out_specs=[pl.BlockSpec(memory_space=pltpu.VMEM)] * len(outputs),
        scratch_shapes=scratch,
        compiler_params=pltpu.CompilerParams(vmem_limit_bytes=VMEM_LIMIT),
    )(*blocks)


def exchange(value, axis, distance):
    count = lax.axis_size(axis)
    return lax.ppermute(value, axis, [(n, n ^ distance) for n in range(count)])


def exchange_groups(rows, columns, mask):
    return [
        [
            ((row ^ mask) * columns + (column ^ FAR_COLUMN)) * 2 + core
            for row in range(rows)
            for column in range(columns)
        ]
        for core in range(2)
    ]


def gather_groups(rows, columns):
    place = lambda row, column, core: (row * columns + column) * 2 + core
    first = [
        [place(row, column ^ FAR_COLUMN, 1) for column in range(columns)] for row in range(rows)
    ]
    second = [
        [place(row ^ GATHER_ROW, column + n, 0) for n in range(2) for row in range(rows)]
        for column in range(0, columns, 2)
    ]
    return first + second


def per_device(
    pair,
    alignment_left,
    alignment_right,
    outer_mean_weight,
    outer_mean_bias,
    input_norm_gain,
    input_norm_bias,
    input_weight_matrix,
    input_bias_vector,
    output_norm_gain,
    output_norm_bias,
    output_weight_matrix,
    output_bias_vector,
):
    rows, columns = lax.axis_size("row"), lax.axis_size("col")

    def spread(value, groups):
        return lax.all_to_all(
            value, ("row", "col", "seq"), 0, 0, tiled=True, axis_index_groups=groups
        )

    core = lax.axis_index("seq")
    left = alignment_left.transpose(1, 2, 0).reshape(64, 64)
    right = alignment_right.transpose(1, 2, 0).reshape(64, 64)
    kept = jnp.where(core == 0, right, left)
    vectors = [
        outer_mean_bias,
        input_norm_gain,
        input_norm_bias,
        output_norm_gain,
        output_norm_bias,
        output_bias_vector,
        input_bias_vector,
    ]
    vectors = jnp.concatenate([vector.reshape(-1, LANES) for vector in vectors], axis=0)
    (blocks,) = call(
        pack_kernel,
        [(1024, LANES)],
        [],
        kept,
        exchange(left, "seq", 1),
        exchange(right, "seq", 1),
    )
    own = spread(blocks, gather_groups(rows, columns))
    send, updated, gate = call(
        tile_kernel,
        [(512, LANES), (256, LANES), (256, LANES)],
        [
            pltpu.VMEM((256, LANES), jnp.float32),
            pltpu.VMEM((256, 1024), jnp.bfloat16),
            pltpu.VMEM((256, 1024), jnp.bfloat16),
        ],
        own,
        exchange(own, "seq", 1),
        pair.reshape(256, LANES),
        outer_mean_weight,
        input_weight_matrix,
        vectors,
    )
    own = spread(send, exchange_groups(rows, columns, OUT_ROW))
    (back,) = call(
        triangle_kernel,
        [(256, LANES)],
        [
            pltpu.VMEM((2, 256, LANES), jnp.float32),
            pltpu.VMEM((2, 128, LANES), jnp.float32),
        ],
        own,
        exchange(own, "seq", 1),
    )
    mixed = spread(back, exchange_groups(rows, columns, BACK_ROW))
    (out,) = call(
        output_kernel,
        [(256, LANES)],
        [],
        mixed,
        updated,
        gate,
        output_weight_matrix,
        vectors,
    )
    return out.reshape(pair.shape)


def solution(mesh):
    return jax.shard_map(
        per_device,
        mesh=mesh,
        in_specs=(
            P("row", ("col", "seq"), None),
            P("seq", "row", "col"),
            P("seq", "col", "row"),
            P(),
            P(),
            P(),
            P(),
            P(),
            P(),
            P(),
            P(),
            P(),
            P(),
        ),
        out_specs=P("row", ("col", "seq"), None),
        check_vma=False,
    )
```

```python
import functools

import jax
import jax.numpy as jnp
from jax import lax
from jax.experimental import pallas as pl
from jax.experimental.pallas import tpu as pltpu
from jax.sharding import PartitionSpec as P

SEQUENCE_COUNT = 128
EPSILON = 1e-05
LANES = 128
VMEM_LIMIT = 32 * 1024 * 1024
GATHER_ROW, OUT_ROW, BACK_ROW, FAR_COLUMN = 5, 7, 6, 10


def split(value):
    high = value.astype(jnp.bfloat16)
    return high, (value - high.astype(jnp.float32)).astype(jnp.bfloat16)


def product(left, right, transposed):
    dims = (((1,), (1 if transposed else 0,)), ((), ()))
    dot = functools.partial(
        lax.dot_general, dimension_numbers=dims, preferred_element_type=jnp.float32
    )
    if left[0].shape[1] == LANES:
        return dot(
            jnp.concatenate([left[0], left[1], left[0]], axis=1),
            jnp.concatenate([right[0], right[0], right[1]], axis=1 if transposed else 0),
        )
    if right[0].shape[1] == LANES and not transposed:
        both = dot(left[0], jnp.concatenate([right[0], right[1]], axis=1))
        return both[:, :LANES] + (both[:, LANES:] + dot(left[1], right[0]))
    return dot(left[0], right[0]) + (dot(left[0], right[1]) + dot(left[1], right[0]))


def swap_groups(blocks):
    lane = lax.broadcasted_iota(jnp.int32, blocks[0].shape, 1)
    wide, narrow = (lane & 64) == 0, (lane & 32) == 0

    def exchange(first, second, shift, mask):
        return (
            jnp.where(mask, first, pltpu.roll(second, shift, 1)),
            jnp.where(mask, pltpu.roll(first, LANES - shift, 1), second),
        )

    a, c = exchange(blocks[0], blocks[2], 64, wide)
    b, d = exchange(blocks[1], blocks[3], 64, wide)
    a, b = exchange(a, b, 32, narrow)
    c, d = exchange(c, d, 32, narrow)
    return a, b, c, d


def pack_kernel(kept_ref, left_ref, right_ref, out_ref):
    first_core = lax.axis_index("seq") == 0

    def ordered(left_ref, right_ref):
        left = [left_ref[pl.ds(p, 32, stride=2), :] for p in range(2)]
        right = [right_ref[pl.ds(q, 16, stride=4), :] for q in range(4)]
        return jnp.where(first_core, jnp.concatenate(right, axis=0), jnp.concatenate(left, axis=0))

    kept, got = ordered(kept_ref, kept_ref), ordered(left_ref, right_ref)
    lower, upper = jnp.where(first_core, kept, got), jnp.where(first_core, got, kept)
    block = jnp.concatenate([lower, upper], axis=1)
    for n in range(16):
        out_ref[pl.ds(n * 64, 64), :] = block


def weights_kernel(own_ref, mean_weight_ref, weight_ref, right_ref, mean_joined_ref, joined_ref):
    core, odd = lax.axis_index("seq"), lax.rem(lax.axis_index("col"), 2)
    for row in range(8):
        for q in range(4):
            start = odd * 512 + row * 64 + q * 16 + core * 8
            rows = pl.ds(pl.multiple_of(start, 8), 8)
            right_ref[pl.ds((row ^ GATHER_ROW) * 32 + q * 8, 8), :] = own_ref[rows, :]
    high, low = split(mean_weight_ref[...])
    mean_joined_ref[...] = jnp.concatenate([high, low], axis=1)
    high, low = split(weight_ref[...])
    joined_ref[...] = jnp.concatenate([high, high, low], axis=0)


def tile_kernel(
    own_ref,
    other_ref,
    pair_ref,
    right_ref,
    mean_joined_ref,
    joined_ref,
    vectors_ref,
    send_ref,
    updated_ref,
    gate_ref,
    right_scratch,
    high_scratch,
    low_scratch,
):
    core, odd = lax.axis_index("seq"), lax.rem(lax.axis_index("col"), 2)
    first_core = core == 0
    for row in range(8):
        for q in range(4):
            start = odd * 512 + row * 64 + q * 16 + core * 8
            rows = pl.ds(pl.multiple_of(start, 8), 8)
            target = pl.ds((row ^ GATHER_ROW) * 32 + q * 8, 8)
            right_scratch[target, :] = jnp.where(
                first_core, right_ref[target, :], other_ref[rows, :]
            )
    right = split(
        jnp.concatenate([right_scratch[pl.ds(j, 32, stride=8), :] for j in range(8)], axis=0)
    )
    left = jnp.where(first_core, other_ref[...], own_ref[...])
    outer = [product(split(left[n * 512 : (n + 1) * 512]), right, True) for n in range(2)]
    for group in range(8):
        for wide in range(2):
            blocks = [
                outer[group // 4][
                    (group % 4 * 4 + p) * 32 : (group % 4 * 4 + p + 1) * 32,
                    wide * LANES : (wide + 1) * LANES,
                ]
                for p in range(4)
            ]
            for j, block in enumerate(swap_groups(blocks)):
                rows = pl.ds((wide * 4 + j) * 32, 32)
                columns = pl.ds((group ^ (FAR_COLUMN // 2)) * LANES, LANES)
                high, low = split(block)
                high_scratch[rows, columns] = high
                low_scratch[rows, columns] = low
    both = jnp.dot(
        high_scratch[...], mean_joined_ref[...], preferred_element_type=jnp.float32
    )
    rest = jnp.dot(
        low_scratch[...], mean_joined_ref[:, :LANES], preferred_element_type=jnp.float32
    )
    summed = both[:, :LANES] + (both[:, LANES:] + rest)
    pair = jnp.concatenate([pair_ref[pl.ds(j, 32, stride=8), :] for j in range(8)], axis=0)
    updated = pair + (summed + vectors_ref[0:1]) * (1.0 / SEQUENCE_COUNT)
    updated_ref[...] = updated
    center = updated - jnp.mean(updated, axis=1, keepdims=True)
    spread = jnp.mean(center * center, axis=1, keepdims=True)
    normed = center * lax.rsqrt(spread + EPSILON) * vectors_ref[1:2] + vectors_ref[2:3]
    high, low = split(normed)
    proj = jnp.dot(
        jnp.concatenate([high, low, high], axis=1),
        joined_ref[...],
        preferred_element_type=jnp.float32,
    )
    blocks = [
        proj[:, n * LANES : (n + 1) * LANES] + vectors_ref[6 + n : 7 + n] for n in range(5)
    ]
    left_act = jnp.transpose(jax.nn.sigmoid(blocks[1]) * blocks[0])
    right_act = jnp.transpose(jax.nn.sigmoid(blocks[3]) * blocks[2])
    for n in range(8):
        channels = slice(n * 16, (n + 1) * 16)
        begin = (n ^ OUT_ROW ^ BACK_ROW) * 64
        send_ref[pl.ds(begin, 16, stride=4), :] = left_act[channels, :LANES]
        send_ref[pl.ds(begin + 1, 16, stride=4), :] = left_act[channels, LANES:]
        send_ref[pl.ds(begin + 2, 16, stride=4), :] = right_act[channels, :LANES]
        send_ref[pl.ds(begin + 3, 16, stride=4), :] = right_act[channels, LANES:]
    gate_ref[...] = jax.nn.sigmoid(blocks[4])


def regroup(ref, part, wide):
    return swap_groups([ref[pl.ds((wide * 4 + r) * 64 + part, 16, stride=4), :] for r in range(4)])


def regroup_kernel(own_ref, left_ref, right_ref):
    for wide in range(2):
        for part in range(2):
            for g, block in enumerate(regroup(own_ref, part, wide)):
                left_ref[pl.ds((wide * 8 + part * 4 + g) * 16, 16), :] = block
            for g, block in enumerate(regroup(own_ref, part + 2, wide)):
                right_ref[pl.ds((wide * 8 + part * 4 + g) * 16, 16), :] = block


def triangle_kernel(left_ref, right_ref, other_ref, send_ref, left_scratch):
    first_core = lax.axis_index("seq") == 0
    for wide in range(2):
        for part in range(2):
            for g, other in enumerate(regroup(other_ref, part, wide)):
                place = part * 4 + g
                own = left_ref[pl.ds((wide * 8 + place) * 16, 16), :]
                lower = jnp.where(first_core, own, other)
                upper = jnp.where(first_core, other, own)
                left_scratch[wide, pl.ds(place, 16, stride=16), :] = lower
                left_scratch[wide, pl.ds(place + 8, 16, stride=16), :] = upper
    left = split(jnp.concatenate([left_scratch[0], left_scratch[1]], axis=1))
    right = split(jnp.concatenate([right_ref[:LANES], right_ref[LANES:]], axis=1))
    mixed = product(right, left, True)
    for wide in range(2):
        for part in range(2):
            blocks = [
                mixed[
                    (part * 4 + g) * 16 : (part * 4 + g + 1) * 16,
                    wide * LANES : (wide + 1) * LANES,
                ]
                for g in range(4)
            ]
            for r, block in enumerate(swap_groups(blocks)):
                place = (wide * 4 + r) ^ (FAR_COLUMN // 2) ^ BACK_ROW
                send_ref[pl.ds(place * 32 + part, 16, stride=2), :] = block


def output_kernel(mixed_ref, updated_ref, gate_ref, weight_ref, vectors_ref, out_ref):
    mixed = jnp.concatenate(
        [mixed_ref[pl.ds(0, 128, stride=2), :], mixed_ref[pl.ds(1, 128, stride=2), :]], axis=1
    )
    center = mixed - jnp.mean(mixed, axis=0, keepdims=True)
    spread = jnp.mean(center * center, axis=0, keepdims=True)
    normed = jnp.transpose(center * lax.rsqrt(spread + EPSILON))
    normed = normed * vectors_ref[3:4] + vectors_ref[4:5]
    result = product(split(normed), split(weight_ref[...]), False) + vectors_ref[5:6]
    out = updated_ref[...] + gate_ref[...] * result
    for j in range(8):
        out_ref[pl.ds(j, 32, stride=8), :] = out[j * 32 : (j + 1) * 32]


def call(kernel, outputs, scratch, *blocks):
    return pl.pallas_call(
        kernel,
        out_shape=[jax.ShapeDtypeStruct(shape, jnp.float32) for shape in outputs],
        in_specs=[pl.BlockSpec(memory_space=pltpu.VMEM)] * len(blocks),
        out_specs=[pl.BlockSpec(memory_space=pltpu.VMEM)] * len(outputs),
        scratch_shapes=scratch,
        compiler_params=pltpu.CompilerParams(vmem_limit_bytes=VMEM_LIMIT),
    )(*blocks)


def exchange(value, axis, distance):
    count = lax.axis_size(axis)
    return lax.ppermute(value, axis, [(n, n ^ distance) for n in range(count)])


def exchange_groups(rows, columns, mask):
    return [
        [
            ((row ^ mask) * columns + (column ^ FAR_COLUMN)) * 2 + core
            for row in range(rows)
            for column in range(columns)
        ]
        for core in range(2)
    ]


def gather_groups(rows, columns):
    place = lambda row, column, core: (row * columns + column) * 2 + core
    first = [
        [place(row, column ^ FAR_COLUMN, 1) for column in range(columns)] for row in range(rows)
    ]
    second = [
        [place(row ^ GATHER_ROW, column + n, 0) for n in range(2) for row in range(rows)]
        for column in range(0, columns, 2)
    ]
    return first + second


def per_device(
    pair,
    alignment_left,
    alignment_right,
    outer_mean_weight,
    outer_mean_bias,
    input_norm_gain,
    input_norm_bias,
    input_weight_matrix,
    input_bias_vector,
    output_norm_gain,
    output_norm_bias,
    output_weight_matrix,
    output_bias_vector,
):
    rows, columns = lax.axis_size("row"), lax.axis_size("col")

    def spread(value, groups):
        return lax.all_to_all(
            value, ("row", "col", "seq"), 0, 0, tiled=True, axis_index_groups=groups
        )

    core = lax.axis_index("seq")
    left = alignment_left.transpose(1, 2, 0).reshape(64, 64)
    right = alignment_right.transpose(1, 2, 0).reshape(64, 64)
    kept = jnp.where(core == 0, right, left)
    vectors = [
        outer_mean_bias,
        input_norm_gain,
        input_norm_bias,
        output_norm_gain,
        output_norm_bias,
        output_bias_vector,
        input_bias_vector,
    ]
    vectors = jnp.concatenate([vector.reshape(-1, LANES) for vector in vectors], axis=0)
    (blocks,) = call(
        pack_kernel,
        [(1024, LANES)],
        [],
        kept,
        exchange(left, "seq", 1),
        exchange(right, "seq", 1),
    )
    own = spread(blocks, gather_groups(rows, columns))
    other = exchange(own, "seq", 1)
    halves = pl.pallas_call(
        weights_kernel,
        out_shape=[
            jax.ShapeDtypeStruct((256, LANES), jnp.float32),
            jax.ShapeDtypeStruct((1024, 2 * LANES), jnp.bfloat16),
            jax.ShapeDtypeStruct((3 * LANES, 5 * LANES), jnp.bfloat16),
        ],
        in_specs=[pl.BlockSpec(memory_space=pltpu.VMEM)] * 3,
        out_specs=[pl.BlockSpec(memory_space=pltpu.VMEM)] * 3,
        compiler_params=pltpu.CompilerParams(vmem_limit_bytes=VMEM_LIMIT),
    )(own, outer_mean_weight, input_weight_matrix)
    send, updated, gate = call(
        tile_kernel,
        [(512, LANES), (256, LANES), (256, LANES)],
        [
            pltpu.VMEM((256, LANES), jnp.float32),
            pltpu.VMEM((256, 1024), jnp.bfloat16),
            pltpu.VMEM((256, 1024), jnp.bfloat16),
        ],
        own,
        other,
        pair.reshape(256, LANES),
        *halves,
        vectors,
    )
    own = spread(send, exchange_groups(rows, columns, OUT_ROW))
    other = exchange(own, "seq", 1)
    regrouped = call(regroup_kernel, [(256, LANES), (256, LANES)], [], own)
    (back,) = call(
        triangle_kernel,
        [(256, LANES)],
        [pltpu.VMEM((2, 256, LANES), jnp.float32)],
        *regrouped,
        other,
    )
    mixed = spread(back, exchange_groups(rows, columns, BACK_ROW))
    (out,) = call(
        output_kernel,
        [(256, LANES)],
        [],
        mixed,
        updated,
        gate,
        output_weight_matrix,
        vectors,
    )
    return out.reshape(pair.shape)


def solution(mesh):
    return jax.shard_map(
        per_device,
        mesh=mesh,
        in_specs=(
            P("row", ("col", "seq"), None),
            P("seq", "row", "col"),
            P("seq", "col", "row"),
            P(),
            P(),
            P(),
            P(),
            P(),
            P(),
            P(),
            P(),
            P(),
            P(),
        ),
        out_specs=P("row", ("col", "seq"), None),
        check_vma=False,
    )
```

```python
import functools

import jax
import jax.numpy as jnp
from jax import lax
from jax.experimental import pallas as pl
from jax.experimental.pallas import tpu as pltpu
from jax.sharding import PartitionSpec as P

SEQUENCE_COUNT = 128
EPSILON = 1e-05
LANES = 128
VMEM_LIMIT = 32 * 1024 * 1024
GATHER_ROW, OUT_ROW, BACK_ROW, FAR_COLUMN = 5, 7, 6, 10


def split(value):
    high = value.astype(jnp.bfloat16)
    return high, (value - high.astype(jnp.float32)).astype(jnp.bfloat16)


def product(left, right, transposed):
    dims = (((1,), (1 if transposed else 0,)), ((), ()))
    dot = functools.partial(
        lax.dot_general, dimension_numbers=dims, preferred_element_type=jnp.float32
    )
    if left[0].shape[1] == LANES:
        return dot(
            jnp.concatenate([left[0], left[1], left[0]], axis=1),
            jnp.concatenate([right[0], right[0], right[1]], axis=1 if transposed else 0),
        )
    if right[0].shape[1] == LANES and not transposed:
        both = dot(left[0], jnp.concatenate([right[0], right[1]], axis=1))
        return both[:, :LANES] + (both[:, LANES:] + dot(left[1], right[0]))
    return dot(left[0], right[0]) + (dot(left[0], right[1]) + dot(left[1], right[0]))


def swap_groups(blocks):
    lane = lax.broadcasted_iota(jnp.int32, blocks[0].shape, 1)
    wide, narrow = (lane & 64) == 0, (lane & 32) == 0

    def exchange(first, second, shift, mask):
        return (
            jnp.where(mask, first, pltpu.roll(second, shift, 1)),
            jnp.where(mask, pltpu.roll(first, LANES - shift, 1), second),
        )

    a, c = exchange(blocks[0], blocks[2], 64, wide)
    b, d = exchange(blocks[1], blocks[3], 64, wide)
    a, b = exchange(a, b, 32, narrow)
    c, d = exchange(c, d, 32, narrow)
    return a, b, c, d


def pack_kernel(kept_ref, left_ref, right_ref, out_ref):
    first_core = lax.axis_index("seq") == 0

    def ordered(left_ref, right_ref):
        left = [left_ref[pl.ds(p, 32, stride=2), :] for p in range(2)]
        right = [right_ref[pl.ds(q, 16, stride=4), :] for q in range(4)]
        return jnp.where(first_core, jnp.concatenate(right, axis=0), jnp.concatenate(left, axis=0))

    kept, got = ordered(kept_ref, kept_ref), ordered(left_ref, right_ref)
    lower, upper = jnp.where(first_core, kept, got), jnp.where(first_core, got, kept)
    block = jnp.concatenate([lower, upper], axis=1)
    for n in range(16):
        out_ref[pl.ds(n * 64, 64), :] = block


def weights_kernel(own_ref, mean_weight_ref, weight_ref, right_ref, mean_joined_ref, joined_ref):
    core, odd = lax.axis_index("seq"), lax.rem(lax.axis_index("col"), 2)
    for row in range(8):
        for q in range(4):
            start = odd * 512 + row * 64 + q * 16 + core * 8
            rows = pl.ds(pl.multiple_of(start, 8), 8)
            right_ref[pl.ds((row ^ GATHER_ROW) * 32 + q * 8, 8), :] = own_ref[rows, :]
    high, low = split(mean_weight_ref[...])
    mean_joined_ref[...] = jnp.concatenate([high, low], axis=1)
    high, low = split(weight_ref[...])
    joined_ref[...] = jnp.concatenate([high, high, low], axis=0)


def tile_kernel(
    own_ref,
    other_ref,
    pair_ref,
    right_ref,
    mean_joined_ref,
    joined_ref,
    vectors_ref,
    send_ref,
    updated_ref,
    gate_ref,
    right_scratch,
    high_scratch,
    low_scratch,
):
    core, odd = lax.axis_index("seq"), lax.rem(lax.axis_index("col"), 2)
    first_core = core == 0
    for row in range(8):
        for q in range(4):
            start = odd * 512 + row * 64 + q * 16 + core * 8
            rows = pl.ds(pl.multiple_of(start, 8), 8)
            target = pl.ds((row ^ GATHER_ROW) * 32 + q * 8, 8)
            right_scratch[target, :] = jnp.where(
                first_core, right_ref[target, :], other_ref[rows, :]
            )
    right = split(
        jnp.concatenate([right_scratch[pl.ds(j, 32, stride=8), :] for j in range(8)], axis=0)
    )
    left = jnp.where(first_core, other_ref[...], own_ref[...])
    outer = [product(split(left[n * 512 : (n + 1) * 512]), right, True) for n in range(2)]
    for group in range(8):
        for wide in range(2):
            blocks = [
                outer[group // 4][
                    (group % 4 * 4 + p) * 32 : (group % 4 * 4 + p + 1) * 32,
                    wide * LANES : (wide + 1) * LANES,
                ]
                for p in range(4)
            ]
            for j, block in enumerate(swap_groups(blocks)):
                rows = pl.ds((wide * 4 + j) * 32, 32)
                columns = pl.ds((group ^ (FAR_COLUMN // 2)) * LANES, LANES)
                high, low = split(block)
                high_scratch[rows, columns] = high
                low_scratch[rows, columns] = low
    both = jnp.dot(
        high_scratch[...], mean_joined_ref[...], preferred_element_type=jnp.float32
    )
    rest = jnp.dot(
        low_scratch[...], mean_joined_ref[:, :LANES], preferred_element_type=jnp.float32
    )
    summed = both[:, :LANES] + (both[:, LANES:] + rest)
    pair = jnp.concatenate([pair_ref[pl.ds(j, 32, stride=8), :] for j in range(8)], axis=0)
    updated = pair + (summed + vectors_ref[0:1]) * (1.0 / SEQUENCE_COUNT)
    updated_ref[...] = updated
    center = updated - jnp.mean(updated, axis=1, keepdims=True)
    spread = jnp.mean(center * center, axis=1, keepdims=True)
    normed = center * lax.rsqrt(spread + EPSILON) * vectors_ref[1:2] + vectors_ref[2:3]
    high, low = split(normed)
    proj = jnp.dot(
        jnp.concatenate([high, low, high], axis=1),
        joined_ref[...],
        preferred_element_type=jnp.float32,
    )
    blocks = [
        proj[:, n * LANES : (n + 1) * LANES] + vectors_ref[6 + n : 7 + n] for n in range(5)
    ]
    left_act = jnp.transpose(jax.nn.sigmoid(blocks[1]) * blocks[0])
    right_act = jnp.transpose(jax.nn.sigmoid(blocks[3]) * blocks[2])
    for n in range(8):
        channels = slice(n * 16, (n + 1) * 16)
        begin = (n ^ OUT_ROW ^ BACK_ROW) * 64
        send_ref[pl.ds(begin, 16, stride=4), :] = left_act[channels, :LANES]
        send_ref[pl.ds(begin + 1, 16, stride=4), :] = left_act[channels, LANES:]
        send_ref[pl.ds(begin + 2, 16, stride=4), :] = right_act[channels, :LANES]
        send_ref[pl.ds(begin + 3, 16, stride=4), :] = right_act[channels, LANES:]
    gate_ref[...] = jax.nn.sigmoid(blocks[4])


def regroup(ref, part, wide):
    return swap_groups([ref[pl.ds((wide * 4 + r) * 64 + part, 16, stride=4), :] for r in range(4)])


def regroup_kernel(own_ref, left_ref, right_ref):
    for wide in range(2):
        for part in range(2):
            for g, block in enumerate(regroup(own_ref, part, wide)):
                left_ref[pl.ds((wide * 8 + part * 4 + g) * 16, 16), :] = block
            for g, block in enumerate(regroup(own_ref, part + 2, wide)):
                right_ref[pl.ds((wide * 8 + part * 4 + g) * 16, 16), :] = block


def triangle_kernel(left_ref, right_ref, other_ref, send_ref, left_scratch):
    first_core = lax.axis_index("seq") == 0
    for wide in range(2):
        for part in range(2):
            for g, other in enumerate(regroup(other_ref, part, wide)):
                place = part * 4 + g
                own = left_ref[pl.ds((wide * 8 + place) * 16, 16), :]
                lower = jnp.where(first_core, own, other)
                upper = jnp.where(first_core, other, own)
                left_scratch[wide, pl.ds(place, 16, stride=16), :] = lower
                left_scratch[wide, pl.ds(place + 8, 16, stride=16), :] = upper
    left = split(jnp.concatenate([left_scratch[0], left_scratch[1]], axis=1))
    right = split(jnp.concatenate([right_ref[:LANES], right_ref[LANES:]], axis=1))
    mixed = product(right, left, True)
    for wide in range(2):
        for part in range(2):
            blocks = [
                mixed[
                    (part * 4 + g) * 16 : (part * 4 + g + 1) * 16,
                    wide * LANES : (wide + 1) * LANES,
                ]
                for g in range(4)
            ]
            for r, block in enumerate(swap_groups(blocks)):
                place = (wide * 4 + r) ^ (FAR_COLUMN // 2) ^ BACK_ROW
                send_ref[pl.ds(place * 32 + part, 16, stride=2), :] = block


def output_kernel(mixed_ref, updated_ref, gate_ref, weight_ref, vectors_ref, out_ref, held_ref, semaphores):
    mixed = jnp.concatenate(
        [mixed_ref[pl.ds(0, 128, stride=2), :], mixed_ref[pl.ds(1, 128, stride=2), :]], axis=1
    )
    center = mixed - jnp.mean(mixed, axis=0, keepdims=True)
    spread = jnp.mean(center * center, axis=0, keepdims=True)
    normed = jnp.transpose(center * lax.rsqrt(spread + EPSILON))
    normed = normed * vectors_ref[3:4] + vectors_ref[4:5]
    result = product(split(normed), split(weight_ref[...]), False) + vectors_ref[5:6]
    out = updated_ref[...] + gate_ref[...] * result
    copies = []
    for part in range(2):
        for j in range(8):
            begin = j * 32 + part * 16
            held_ref[pl.ds(part * 128 + j, 16, stride=8), :] = out[begin : begin + 16]
        rows = pl.ds(part * 128, 128)
        copies.append(pltpu.make_async_copy(held_ref.at[rows], out_ref.at[rows], semaphores.at[part]))
        copies[-1].start()
    for copy in copies:
        copy.wait()


def call(kernel, outputs, scratch, *blocks):
    return pl.pallas_call(
        kernel,
        out_shape=[jax.ShapeDtypeStruct(shape, jnp.float32) for shape in outputs],
        in_specs=[pl.BlockSpec(memory_space=pltpu.VMEM)] * len(blocks),
        out_specs=[pl.BlockSpec(memory_space=pltpu.VMEM)] * len(outputs),
        scratch_shapes=scratch,
        compiler_params=pltpu.CompilerParams(vmem_limit_bytes=VMEM_LIMIT),
    )(*blocks)


def exchange(value, axis, distance):
    count = lax.axis_size(axis)
    return lax.ppermute(value, axis, [(n, n ^ distance) for n in range(count)])


def exchange_groups(rows, columns, mask):
    return [
        [
            ((row ^ mask) * columns + (column ^ FAR_COLUMN)) * 2 + core
            for row in range(rows)
            for column in range(columns)
        ]
        for core in range(2)
    ]


def gather_groups(rows, columns):
    place = lambda row, column, core: (row * columns + column) * 2 + core
    first = [
        [place(row, column ^ FAR_COLUMN, 1) for column in range(columns)] for row in range(rows)
    ]
    second = [
        [place(row ^ GATHER_ROW, column + n, 0) for n in range(2) for row in range(rows)]
        for column in range(0, columns, 2)
    ]
    return first + second


def per_device(
    pair,
    alignment_left,
    alignment_right,
    outer_mean_weight,
    outer_mean_bias,
    input_norm_gain,
    input_norm_bias,
    input_weight_matrix,
    input_bias_vector,
    output_norm_gain,
    output_norm_bias,
    output_weight_matrix,
    output_bias_vector,
):
    rows, columns = lax.axis_size("row"), lax.axis_size("col")

    def spread(value, groups):
        return lax.all_to_all(
            value, ("row", "col", "seq"), 0, 0, tiled=True, axis_index_groups=groups
        )

    core = lax.axis_index("seq")
    left = alignment_left.transpose(1, 2, 0).reshape(64, 64)
    right = alignment_right.transpose(1, 2, 0).reshape(64, 64)
    kept = jnp.where(core == 0, right, left)
    vectors = [
        outer_mean_bias,
        input_norm_gain,
        input_norm_bias,
        output_norm_gain,
        output_norm_bias,
        output_bias_vector,
        input_bias_vector,
    ]
    vectors = jnp.concatenate([vector.reshape(-1, LANES) for vector in vectors], axis=0)
    (blocks,) = call(
        pack_kernel,
        [(1024, LANES)],
        [],
        kept,
        exchange(left, "seq", 1),
        exchange(right, "seq", 1),
    )
    own = spread(blocks, gather_groups(rows, columns))
    other = exchange(own, "seq", 1)
    halves = pl.pallas_call(
        weights_kernel,
        out_shape=[
            jax.ShapeDtypeStruct((256, LANES), jnp.float32),
            jax.ShapeDtypeStruct((1024, 2 * LANES), jnp.bfloat16),
            jax.ShapeDtypeStruct((3 * LANES, 5 * LANES), jnp.bfloat16),
        ],
        in_specs=[pl.BlockSpec(memory_space=pltpu.VMEM)] * 3,
        out_specs=[pl.BlockSpec(memory_space=pltpu.VMEM)] * 3,
        compiler_params=pltpu.CompilerParams(vmem_limit_bytes=VMEM_LIMIT),
    )(own, outer_mean_weight, input_weight_matrix)
    send, updated, gate = call(
        tile_kernel,
        [(512, LANES), (256, LANES), (256, LANES)],
        [
            pltpu.VMEM((256, LANES), jnp.float32),
            pltpu.VMEM((256, 1024), jnp.bfloat16),
            pltpu.VMEM((256, 1024), jnp.bfloat16),
        ],
        own,
        other,
        pair.reshape(256, LANES),
        *halves,
        vectors,
    )
    own = spread(send, exchange_groups(rows, columns, OUT_ROW))
    other = exchange(own, "seq", 1)
    regrouped = call(regroup_kernel, [(256, LANES), (256, LANES)], [], own)
    (back,) = call(
        triangle_kernel,
        [(256, LANES)],
        [pltpu.VMEM((2, 256, LANES), jnp.float32)],
        *regrouped,
        other,
    )
    mixed = spread(back, exchange_groups(rows, columns, BACK_ROW))
    out = pl.pallas_call(
        output_kernel,
        out_shape=jax.ShapeDtypeStruct((256, LANES), jnp.float32),
        in_specs=[pl.BlockSpec(memory_space=pltpu.VMEM)] * 5,
        out_specs=pl.BlockSpec(memory_space=pltpu.HBM),
        scratch_shapes=[pltpu.VMEM((256, LANES), jnp.float32), pltpu.SemaphoreType.DMA((2,))],
        compiler_params=pltpu.CompilerParams(vmem_limit_bytes=VMEM_LIMIT),
    )(mixed, updated, gate, output_weight_matrix, vectors)
    return out.reshape(pair.shape)


def solution(mesh):
    return jax.shard_map(
        per_device,
        mesh=mesh,
        in_specs=(
            P("row", ("col", "seq"), None),
            P("seq", "row", "col"),
            P("seq", "col", "row"),
            P(),
            P(),
            P(),
            P(),
            P(),
            P(),
            P(),
            P(),
            P(),
            P(),
        ),
        out_specs=P("row", ("col", "seq"), None),
        check_vma=False,
    )
```
